256 devices in a mesh: pb: 8 (over x_lo, y), kv: 32 (over x_hi, z, core).
Axes of the slice: x: 4 (x_hi: 2, x_lo: 2; x = x_hi * 2 + x_lo), y: 4, z: 8, core: 2. Of those that a mesh axis runs over, the one named last changes fastest.
Arguments:
- queries: bfloat16 [131072, 1024], P(('pb', 'kv')), may hold values from -33 to 33
- keys: bfloat16 [131072, 1024], P(('pb', 'kv')), may hold values from -33 to 33
- values: bfloat16 [131072, 1024], P(('pb', 'kv')), may hold values from -6 to 6
- grad_out: bfloat16 [131072, 1024], P(('pb', 'kv')), may hold values from -6 to 6
- offsets: int32 [256, 5], P(('pb', 'kv')), may hold values from -2 to 3, as said below
Outputs:
- grad_queries: float32 [131072, 1024], P(('pb', 'kv'))
- grad_keys: float32 [131072, 1024], P(('pb', 'kv'))
- grad_values: float32 [131072, 1024], P(('pb', 'kv'))
The draws below stay inside these ranges and needn't reach their ends.
Inputs may be any that keep to these rules, and one draw needn't show every extreme that they name: `offsets`: slot s holds s - 2 if the query block attends the node block at that offset, else 3; slot 2 always holds 0; an offset that leaves the blocks 0 to 255 is never attended.
All inputs are finite; a program needn't handle non-finite values.
Results may differ from the reference program's by a relative error of at most 0.0045.
Values may be sent and summed in bfloat16 or wider, within the bound.
A program may use at most 192 MiB of HBM per device.

```python
import jax
import jax.numpy as jnp
from jax import lax

HEADS = 8
HEAD_DIM = 128
BLOCK = 512
BAND = 5
D = 1024
NBLK = 256
TOKENS = 131072


def draw_queries(key, part):
    key = jax.random.fold_in(key, 1)
    return jnp.clip(jax.random.normal(key, (TOKENS, D), jnp.float32), -6.0, 6.0).astype(jnp.bfloat16)


def draw_keys(key, part):
    key = jax.random.fold_in(key, 2)
    return jnp.clip(jax.random.normal(key, (TOKENS, D), jnp.float32), -6.0, 6.0).astype(jnp.bfloat16)


def draw_offsets(key, part):
    key = jax.random.fold_in(key, 7)
    draws_kept = jax.random.randint(key, (NBLK, BAND), 0, 4)
    slot_offsets = jnp.arange(BAND, dtype=jnp.int32)[None, :] - 2
    target_block = jnp.arange(NBLK, dtype=jnp.int32)[:, None] + slot_offsets
    inside = (target_block >= 0) & (target_block < NBLK)
    attend_flags = inside & ((draws_kept != 0) | (slot_offsets == 0))
    return jnp.where(attend_flags, slot_offsets, 3).astype(jnp.int32)


def shard_levels(key, shape, split, smallest, top_value):
    gain = 1.0
    for axis_at, shards_of in split:
        draws = jax.random.uniform(jax.random.fold_in(jax.random.fold_in(key, 6), axis_at), (shards_of,), jnp.float32, smallest / len(split), top_value / len(split))
        gain = gain * jnp.repeat(jnp.exp(draws), shape[axis_at] // shards_of).reshape((-1,) + (1,) * (len(shape) - 1 - axis_at))
    return gain


def gaussian(own_key, extent, spread, bound, cuts=(), kind=jnp.bfloat16):
    loudness = shard_levels(own_key, extent, cuts, -0.22, 0.18) if cuts else 1.0
    array = jax.random.normal(own_key, extent, jnp.float32) * spread * loudness
    return jnp.minimum(jnp.maximum(array, -bound), bound).astype(kind)


def setup_inputs(seed: int = 0) -> dict:
    seeds = jax.random.split(jax.random.key(seed), 6)
    return {
        "queries": draw_queries(jax.random.fold_in(seeds[5], 71), 0),
        "keys": draw_keys(jax.random.fold_in(seeds[5], 71), 0),
        "values": gaussian(seeds[2], (TOKENS, D), 1.0, 6.0, ((0, 256),)),
        "grad_out": gaussian(seeds[3], (TOKENS, D), 1.0, 6.0, ((0, 256),)),
        "offsets": draw_offsets(jax.random.fold_in(seeds[5], 71), 0),
    }


NEG_FILL = -1.0e30


def block_grads(query_block, key_blocks, value_blocks, grad_block, attended):
    softmax_scale = HEAD_DIM ** -0.5
    query_heads = query_block.astype(jnp.float32).reshape(BLOCK, HEADS, HEAD_DIM)
    key_heads = key_blocks.astype(jnp.float32).reshape(BAND, BLOCK, HEADS, HEAD_DIM)
    value_heads = value_blocks.astype(jnp.float32).reshape(BAND, BLOCK, HEADS, HEAD_DIM)
    grad_heads = grad_block.astype(jnp.float32).reshape(BLOCK, HEADS, HEAD_DIM)
    scores = jnp.einsum("qhd,skhd->hqsk", query_heads, key_heads) * softmax_scale
    scores = jnp.where(attended[None, None, :, None], scores, NEG_FILL)
    row_max = jnp.max(scores, axis=(2, 3), keepdims=True)
    log_total = row_max + jnp.log(jnp.sum(jnp.exp(scores - row_max), axis=(2, 3), keepdims=True))
    weights = jnp.exp(scores - log_total)
    grad_weights = jnp.einsum("qhd,skhd->hqsk", grad_heads, value_heads)
    row_dot = jnp.sum(weights * grad_weights, axis=(2, 3), keepdims=True)
    grad_scores = lax.optimization_barrier((weights * (grad_weights - row_dot)).astype(jnp.bfloat16)).astype(jnp.float32)
    weights_low = lax.optimization_barrier(weights.astype(jnp.bfloat16)).astype(jnp.float32)
    grad_query = jnp.einsum("hqsk,skhd->qhd", grad_scores, key_heads) * softmax_scale
    grad_key = jnp.einsum("hqsk,qhd->skhd", grad_scores, query_heads) * softmax_scale
    grad_value = jnp.einsum("hqsk,qhd->skhd", weights_low, grad_heads)
    return grad_query.reshape(BLOCK, D), grad_key.reshape(BAND, BLOCK, D), grad_value.reshape(BAND, BLOCK, D)


def reference(queries, keys, values, grad_out, offsets):
    padded_keys = jnp.pad(keys.reshape(NBLK, BLOCK, D), ((2, 2), (0, 0), (0, 0)))
    padded_values = jnp.pad(values.reshape(NBLK, BLOCK, D), ((2, 2), (0, 0), (0, 0)))
    key_total = jnp.zeros((NBLK + 4, BLOCK, D), jnp.float32)
    value_total = jnp.zeros((NBLK + 4, BLOCK, D), jnp.float32)

    def advance(carry, inputs):
        key_sum, value_sum = carry
        block_index, query_block, grad_block, offset_row = inputs
        anchor = jnp.zeros((), jnp.int32)
        start = (block_index.astype(jnp.int32), anchor, anchor)
        key_blocks = lax.dynamic_slice(padded_keys, start, (BAND, BLOCK, D))
        value_blocks = lax.dynamic_slice(padded_values, start, (BAND, BLOCK, D))
        attended = offset_row != 3
        grad_query, grad_key, grad_value = block_grads(query_block, key_blocks, value_blocks, grad_block, attended)
        key_sum = lax.dynamic_update_slice(key_sum, lax.dynamic_slice(key_sum, start, (BAND, BLOCK, D)) + grad_key, start)
        value_sum = lax.dynamic_update_slice(value_sum, lax.dynamic_slice(value_sum, start, (BAND, BLOCK, D)) + grad_value, start)
        return (key_sum, value_sum), grad_query

    inputs = (jnp.arange(NBLK, dtype=jnp.int32), queries.reshape(NBLK, BLOCK, D), grad_out.reshape(NBLK, BLOCK, D), offsets)
    (key_total, value_total), grad_blocks = lax.scan(advance, (key_total, value_total), inputs)
    grad_queries = grad_blocks.reshape(TOKENS, D)
    grad_keys = key_total[2:NBLK + 2].reshape(TOKENS, D)
    grad_values = value_total[2:NBLK + 2].reshape(TOKENS, D)
    return (grad_queries, grad_keys, grad_values)
```

```python
import functools
import math

import jax
import jax.numpy as jnp
from jax import lax
from jax.experimental import pallas as pl
from jax.experimental.pallas import tpu as pltpu
from jax.sharding import PartitionSpec as P

HEADS = 8
BAND = 5
HG = HEADS // 2
HD = 128
BLK = 512
R = 256
SPLIT = BLK // R
U = HG * SPLIT
PAIRS = 10
NEG = -1e30
SCALE = HD**-0.5
C2 = SCALE * math.log2(math.e)
MESH = pl.DeviceIdType.MESH
F32, BF16 = jnp.float32, jnp.bfloat16
AHEAD = 2


def nt(a, b):
    return lax.dot_general(a, b, (((1,), (1,)), ((), ())), preferred_element_type=F32)


def nn(a, b):
    return lax.dot_general(a, b, (((1,), (0,)), ((), ())), preferred_element_type=F32)


def tn(a, b):
    return lax.dot_general(a, b, (((0,), (0,)), ((), ())), preferred_element_type=F32)


def kernel(
    pb_size, kv_size,
    q_ref, k_ref, v_ref, do_ref, off_ref,
    dqloc, dql, dqr, dk, dv,
    qd, kv, p, gw, mx, fr, dqj, acc, dqf, dqb, st_s, st_r, ret_s, ret_r, mk,
    qd_rs, kv_rs, st_rs, ret_rs, mk_rs, out_rs, send_s, loc_s,
):
    n = pb_size * kv_size
    me = lax.axis_index("pb") * kv_size + lax.axis_index("kv")
    g = lax.rem(me, 2)
    base = me - g

    def dev(block):
        block = lax.rem(block + n, n)
        return (lax.div(block, kv_size), lax.rem(block, kv_size))

    mate = dev(base + 1 - g)
    left = [dev(base - 2), dev(base - 1)]
    right = [dev(base + 2), dev(base + 3)]
    left_me, right_me = dev(me - 2), dev(me + 2)

    def remote(src, dst, send, recv, to):
        return pltpu.make_async_remote_copy(
            src_ref=src, dst_ref=dst, send_sem=send, recv_sem=recv, device_id=to, device_id_type=MESH
        )

    def wait_bytes(ref, sem):
        pltpu.make_async_copy(ref, ref, sem).wait()

    barrier = pltpu.get_barrier_semaphore()
    for to in [mate] + left + right:
        pl.semaphore_signal(barrier, inc=1, device_id=to, device_id_type=MESH)

    for slot in range(8):
        if slot < BAND:
            flag = jnp.where(off_ref[0, slot] != 3, 1.0, 0.0).astype(F32)
        else:
            flag = jnp.float32(0.0)
        mk[2 + g, slot : slot + 1, :] = jnp.full((1, R), flag, F32)

    def own_copies(u):
        h, half = lax.div(u, SPLIT), lax.rem(u, SPLIT)
        rows = pl.ds(pl.multiple_of(half * R, R), R)
        cols = pl.ds(pl.multiple_of((g * HG + h) * HD, HD), HD)
        return [
            pltpu.make_async_copy(ref.at[rows, cols], qd.at[2 + g, u, i], loc_s.at[0, u])
            for i, ref in enumerate((q_ref, do_ref))
        ]

    def own_kv(h):
        cols = pl.ds(pl.multiple_of((g * HG + h) * HD, HD), HD)
        return [
            pltpu.make_async_copy(ref.at[:, cols], kv.at[h, g, i], loc_s.at[1, h])
            for i, ref in enumerate((k_ref, v_ref))
        ]

    def send_queries(u):
        h, half = lax.div(u, SPLIT), lax.rem(u, SPLIT)
        rows = pl.ds(pl.multiple_of(half * R, R), R)
        mate_cols = pl.ds(pl.multiple_of(((1 - g) * HG + h) * HD, HD), HD)
        for i, ref in enumerate((q_ref, do_ref)):
            remote(
                ref.at[rows, mate_cols], qd.at[2 + g, u, i], send_s.at[0], qd_rs.at[2, u], mate
            ).start()
        for core in range(2):
            cols = pl.ds(pl.multiple_of((core * HG + h) * HD, HD), HD)
            for i, ref in enumerate((q_ref, do_ref)):
                remote(
                    ref.at[rows, cols], qd.at[4 + g, u, i], send_s.at[0], qd_rs.at[3 + g, u], left[core]
                ).start()
                remote(
                    ref.at[rows, cols], qd.at[g, u, i], send_s.at[0], qd_rs.at[g, u], right[core]
                ).start()

    def send_kv(h):
        cols = pl.ds(pl.multiple_of(((1 - g) * HG + h) * HD, HD), HD)
        for i, ref in enumerate((k_ref, v_ref)):
            remote(
                ref.at[:, cols], kv.at[h, g, i], send_s.at[1], kv_rs.at[h], mate
            ).start()

    def start_own(u, carry):
        for copy in own_copies(u):
            copy.start()
        return carry

    def start_own_kv(h, carry):
        for copy in own_kv(h):
            copy.start()
        return carry

    lax.fori_loop(0, HG, start_own_kv, 0)
    lax.fori_loop(0, U, start_own, 0)

    pl.semaphore_wait(barrier, 5)

    send_queries(0)
    send_kv(0)
    tile = mk.at[2 + g]
    remote(tile, mk.at[2 + g], send_s.at[2], mk_rs.at[2], mate).start()
    for core in range(2):
        remote(tile, mk.at[4 + g], send_s.at[2], mk_rs.at[3 + g], left[core]).start()
        remote(tile, mk.at[g], send_s.at[2], mk_rs.at[g], right[core]).start()
    for u in range(1, AHEAD):
        send_queries(u)
    for h in range(1, HG):
        send_kv(h)

    def wait_arrival(u, source):
        t = (0, 1, 3 - g, 4, 5)[source]
        wait_bytes(qd.at[t, u], qd_rs.at[source, u])

    def first_pass(u, par):
        h = lax.div(u, SPLIT)

        def pair(j, carry):
            t, x = lax.div(j + 1, 2), lax.rem(j, 2)
            raw = nt(kv[h, x, 0], qd[t, u, 0])
            m = jnp.max(raw, axis=0, keepdims=True) * C2
            e = jnp.exp2(raw * C2 - m)
            p[par, j] = e
            grads = nt(kv[h, x, 1], qd[t, u, 1])
            gw[par, j] = grads
            mx[par, j, 0:1, :] = m
            mx[par, j, 1:2, :] = jnp.sum(e, axis=0, keepdims=True)
            mx[par, j, 2:3, :] = jnp.sum(e * grads, axis=0, keepdims=True)
            return carry

        return pair

    def attended(t, x):
        return mk[t, 4 - t + x : 5 - t + x, :] > 0.5

    def merge(entries):
        top = functools.reduce(jnp.maximum, [m for m, _, _ in entries])
        weights = [jnp.exp2(m - top) for m, _, _ in entries]
        total = sum(l * w for (_, l, _), w in zip(entries, weights))
        dots = sum(r * w for (_, _, r), w in zip(entries, weights))
        return top, total, dots

    def chip_stats(par, t):
        entries = []
        for x in range(2):
            if (t, x) in ((0, 1), (5, 0)):
                continue
            j = 2 * t - x
            on = attended(t, x)
            m = jnp.where(on, mx[par, j, 0:1, :], NEG)
            l = jnp.where(on, mx[par, j, 1:2, :], 0.0)
            r = jnp.where(on, mx[par, j, 2:3, :], 0.0)
            entries.append((m, l, r))
        return merge(entries)

    def send_stats(u, par):
        for side, ts, to in ((0, (0, 1), left_me), (1, (4, 5), right_me)):
            for i, t in enumerate(ts):
                for row, value in enumerate(chip_stats(par, t)):
                    st_s[u, side, 4 * i + row : 4 * i + row + 1, :] = value
            remote(st_s.at[u, side], st_r.at[u, 1 - side], send_s.at[3], st_rs.at[1 - side, u], to).start()

    def combine(u, par):
        for side in range(2):
            wait_bytes(st_r.at[u, side], st_rs.at[side, u])
        for i, t in enumerate((2, 3)):
            entries = [chip_stats(par, t)]
            for side in range(2):
                entries.append(tuple(st_r[u, side, 4 * i + row : 4 * i + row + 1, :] for row in range(3)))
            top, total, dots = merge(entries)
            ret_s[u, 4 * i : 4 * i + 1, :] = top + jnp.log2(total)
            ret_s[u, 4 * i + 1 : 4 * i + 2, :] = dots / total
        remote(ret_s.at[u], ret_r.at[u, 1], send_s.at[4], ret_rs.at[1, u], left_me).start()
        remote(ret_s.at[u], ret_r.at[u, 0], send_s.at[4], ret_rs.at[0, u], right_me).start()

    def factors(par, t, log_total, row_dot):
        for x in range(2):
            if (t, x) in ((0, 1), (5, 0)):
                continue
            j = 2 * t - x
            power = jnp.where(attended(t, x), mx[par, j, 0:1, :] - log_total, NEG)
            fr[j, 0:1, :] = jnp.exp2(power)
            fr[j, 1:2, :] = row_dot

    def second_pass(u, par):
        h = lax.div(u, SPLIT)

        def pair(j, carry):
            t, x = lax.div(j + 1, 2), lax.rem(j, 2)
            w = p[par, j] * fr[j, 0:1, :]
            low = w.astype(BF16)
            ds = (w * (gw[par, j] - fr[j, 1:2, :])).astype(BF16)
            acc[h, x, 1] += nn(low, qd[t, u, 1])
            acc[h, x, 0] += nn(ds, qd[t, u, 0])
            dqj[j] = tn(ds, kv[h, x, 0])
            return carry

        return pair

    def start_unit(u, par):
        h = lax.div(u, SPLIT)

        @pl.when(u + AHEAD < U)
        def _():
            send_queries(u + AHEAD)

        @pl.when(lax.rem(u, SPLIT) == 0)
        def _():
            wait_bytes(kv.at[h, g], loc_s.at[1, h])
            wait_bytes(kv.at[h, 1 - g], kv_rs.at[h])
            acc[h] = jnp.zeros((2, 2, BLK, HD), F32)

        @pl.when(u == 0)
        def _():
            wait_bytes(mk.at[3 - g], mk_rs.at[2])
            for source, t in ((0, 0), (1, 1), (3, 4), (4, 5)):
                wait_bytes(mk.at[t], mk_rs.at[source])

        wait_bytes(qd.at[2 + g, u], loc_s.at[0, u])
        wait_arrival(u, 2)
        pair = first_pass(u, par)
        lax.fori_loop(3, 7, pair, 0)
        wait_arrival(u, 0)
        wait_arrival(u, 1)
        lax.fori_loop(0, 3, pair, 0)
        wait_arrival(u, 3)
        wait_arrival(u, 4)
        lax.fori_loop(7, 10, pair, 0)
        send_stats(u, par)

    def finish_unit(u, par):
        h, half = lax.div(u, SPLIT), lax.rem(u, SPLIT)
        rows = pl.ds(pl.multiple_of(half * R, R), R)
        cols = pl.ds(pl.multiple_of((g * HG + h) * HD, HD), HD)
        pair = second_pass(u, par)

        wait_bytes(ret_r.at[u, 0], ret_rs.at[0, u])
        for i, t in enumerate((0, 1)):
            factors(par, t, ret_r[u, 0, 4 * i : 4 * i + 1, :], ret_r[u, 0, 4 * i + 1 : 4 * i + 2, :])
        lax.fori_loop(0, 3, pair, 0)
        dqb[u, 0] = dqj[0].astype(BF16)
        dqb[u, 1] = (dqj[1] + dqj[2]).astype(BF16)
        for core in range(2):
            remote(
                dqb.at[u, core], dqr.at[rows, cols], send_s.at[5], out_rs.at[0], left[core]
            ).start()

        wait_bytes(ret_r.at[u, 1], ret_rs.at[1, u])
        for i, t in enumerate((4, 5)):
            factors(par, t, ret_r[u, 1, 4 * i : 4 * i + 1, :], ret_r[u, 1, 4 * i + 1 : 4 * i + 2, :])
        lax.fori_loop(7, 10, pair, 0)
        dqb[u, 2] = (dqj[7] + dqj[8]).astype(BF16)
        dqb[u, 3] = dqj[9].astype(BF16)
        for core in range(2):
            remote(
                dqb.at[u, 2 + core], dql.at[rows, cols], send_s.at[5], out_rs.at[1], right[core]
            ).start()

        for i, t in enumerate((2, 3)):
            factors(par, t, ret_s[u, 4 * i : 4 * i + 1, :], ret_s[u, 4 * i + 1 : 4 * i + 2, :])
        lax.fori_loop(3, 7, pair, 0)
        dqf[u, 0] = dqj[3] + dqj[4]
        dqf[u, 1] = dqj[5] + dqj[6]
        pltpu.make_async_copy(dqf.at[u, g], dqloc.at[rows, cols], loc_s.at[2, 0]).start()
        remote(
            dqf.at[u, 1 - g], dqloc.at[rows, cols], send_s.at[6], out_rs.at[2], mate
        ).start()

        @pl.when(half == SPLIT - 1)
        def _():
            for i, out in enumerate((dk, dv)):
                pltpu.make_async_copy(acc.at[h, g, i], out.at[:, cols], loc_s.at[2, 1 + i]).start()
                remote(
                    acc.at[h, 1 - g, i], out.at[:, cols], send_s.at[7 + i], out_rs.at[3 + i], mate
                ).start()

    def step(s, carry):
        @pl.when(s < U)
        def _():
            start_unit(s, lax.rem(s, 2))

        @pl.when(s >= 1)
        def _():
            finish_unit(s - 1, lax.rem(s - 1, 2))

        @pl.when(s < U)
        def _():
            combine(s, lax.rem(s, 2))

        return carry

    lax.fori_loop(0, U + 1, step, 0)

    mine = pl.ds(pl.multiple_of(g * HG * HD, HD), HG * HD)
    theirs = pl.ds(pl.multiple_of((1 - g) * HG * HD, HD), HG * HD)
    wait_bytes(qd.at[pl.ds(0, 5)], send_s.at[0])
    wait_bytes(kv.at[:, 0], send_s.at[1])
    wait_bytes(mk.at[pl.ds(0, 5)], send_s.at[2])
    wait_bytes(st_s, send_s.at[3])
    wait_bytes(ret_r, send_s.at[4])
    wait_bytes(dqb, send_s.at[5])
    wait_bytes(dqf.at[:, 0], send_s.at[6])
    wait_bytes(acc.at[:, 0, 0], send_s.at[7])
    wait_bytes(acc.at[:, 0, 1], send_s.at[8])
    wait_bytes(dqloc.at[:, mine], loc_s.at[2, 0])
    wait_bytes(dk.at[:, mine], loc_s.at[2, 1])
    wait_bytes(dv.at[:, mine], loc_s.at[2, 2])
    wait_bytes(dqr, out_rs.at[0])
    wait_bytes(dql, out_rs.at[1])
    wait_bytes(dqloc.at[:, theirs], out_rs.at[2])
    wait_bytes(dk.at[:, theirs], out_rs.at[3])
    wait_bytes(dv.at[:, theirs], out_rs.at[4])


def body(pb_size, kv_size, queries, keys, values, grad_out, offsets):
    rows, width = queries.shape
    any_space = pl.BlockSpec(memory_space=pl.ANY)
    whole = jax.ShapeDtypeStruct((rows, width), F32)
    low = jax.ShapeDtypeStruct((rows, width), BF16)
    dma = pltpu.SemaphoreType.DMA
    dqloc, dql, dqr, dk, dv = pl.pallas_call(
        functools.partial(kernel, pb_size, kv_size),
        out_shape=(whole, low, low, whole, whole),
        in_specs=[any_space] * 4 + [pl.BlockSpec(memory_space=pltpu.SMEM)],
        out_specs=[any_space] * 5,
        scratch_shapes=[
            pltpu.VMEM((6, U, 2, R, HD), BF16),
            pltpu.VMEM((HG, 2, 2, BLK, HD), BF16),
            pltpu.VMEM((2, PAIRS, BLK, R), F32),
            pltpu.VMEM((2, PAIRS, BLK, R), F32),
            pltpu.VMEM((2, PAIRS, 8, R), F32),
            pltpu.VMEM((PAIRS, 8, R), F32),
            pltpu.VMEM((PAIRS, R, HD), F32),
            pltpu.VMEM((HG, 2, 2, BLK, HD), F32),
            pltpu.VMEM((U, 2, R, HD), F32),
            pltpu.VMEM((U, 4, R, HD), BF16),
            pltpu.VMEM((U, 2, 8, R), F32),
            pltpu.VMEM((U, 2, 8, R), F32),
            pltpu.VMEM((U, 8, R), F32),
            pltpu.VMEM((U, 2, 8, R), F32),
            pltpu.VMEM((6, 8, R), F32),
            dma((5, U)),
            dma((HG,)),
            dma((2, U)),
            dma((2, U)),
            dma((5,)),
            dma((5,)),
            dma((9,)),
            dma((3, U)),
        ],
        compiler_params=pltpu.CompilerParams(
            collective_id=0, has_side_effects=True, vmem_limit_bytes=56 << 20
        ),
        cost_estimate=pl.CostEstimate(flops=14 * 10**9, bytes_accessed=16 << 20, transcendentals=10 * 2**20),
        name="band_backward",
    )(queries, keys, values, grad_out, offsets)
    grad_queries = (dqloc + dql.astype(F32) + dqr.astype(F32)) * SCALE
    return grad_queries, dk * SCALE, dv


def solution(mesh):
    spec = P(("pb", "kv"), None)
    return jax.shard_map(
        functools.partial(body, mesh.shape["pb"], mesh.shape["kv"]),
        mesh=mesh,
        in_specs=(spec,) * 5,
        out_specs=(spec,) * 3,
        check_vma=False,
    )
```

```python
import functools
import math

import jax
import jax.numpy as jnp
from jax import lax
from jax.experimental import pallas as pl
from jax.experimental.pallas import tpu as pltpu
from jax.sharding import PartitionSpec as P

HEADS = 8
BAND = 5
HG = HEADS // 2
HD = 128
BLK = 512
R = 256
SPLIT = BLK // R
U = HG * SPLIT
PAIRS = 10
NEG = -1e30
SCALE = HD**-0.5
C2 = SCALE * math.log2(math.e)
MESH = pl.DeviceIdType.MESH
F32, BF16 = jnp.float32, jnp.bfloat16
AHEAD = 3
VMEM_LIMIT = 42 << 20


def nt(a, b):
    return lax.dot_general(a, b, (((1,), (1,)), ((), ())), preferred_element_type=F32)


def nn(a, b):
    return lax.dot_general(a, b, (((1,), (0,)), ((), ())), preferred_element_type=F32)


def tn(a, b):
    return lax.dot_general(a, b, (((0,), (0,)), ((), ())), preferred_element_type=F32)


def kernel(
    pb_size, kv_size,
    q_ref, k_ref, v_ref, do_ref, off_ref,
    dq, dk, dv,
    qd, kv, p, gw, mx, fr, dqj, acc, dqf, dqb, dqr, st_s, st_r, ret_s, ret_r, mk, off,
    qd_rs, kv_rs, st_rs, ret_rs, mk_rs, out_rs, send_s, side_s, loc_s, off_s,
):
    n = pb_size * kv_size
    me = lax.axis_index("pb") * kv_size + lax.axis_index("kv")
    g = lax.rem(me, 2)
    base = me - g

    def dev(block):
        block = lax.rem(block + n, n)
        return (lax.div(block, kv_size), lax.rem(block, kv_size))

    present = (base > 0, base + 2 < n)
    mate = dev(base + 1 - g)
    chips = ([dev(base - 2), dev(base - 1)], [dev(base + 2), dev(base + 3)])
    peers = (dev(me - 2), dev(me + 2))
    slots = (4 + g, g)
    theirs_t = ((0, 1), (4, 5))

    def remote(src, dst, send, recv, to):
        return pltpu.make_async_remote_copy(
            src_ref=src, dst_ref=dst, send_sem=send, recv_sem=recv, device_id=to, device_id_type=MESH
        )

    def wait_bytes(ref, sem):
        pltpu.make_async_copy(ref, ref, sem).wait()

    def part(u):
        h, half = lax.div(u, SPLIT), lax.rem(u, SPLIT)
        return h, half, pl.ds(pl.multiple_of(half * R, R), R)

    def head_cols(core, h):
        return pl.ds(pl.multiple_of((core * HG + h) * HD, HD), HD)

    barrier = pltpu.get_barrier_semaphore()
    pl.semaphore_signal(barrier, inc=1, device_id=mate, device_id_type=MESH)
    for side in range(2):

        @pl.when(present[side])
        def _():
            for to in chips[side]:
                pl.semaphore_signal(barrier, inc=1, device_id=to, device_id_type=MESH)

    copy = pltpu.make_async_copy(off_ref, off, off_s.at[0])
    copy.start()
    copy.wait()
    for slot in range(8):
        if slot < BAND:
            flag = jnp.where(off[0, slot] != 3, 1.0, 0.0).astype(F32)
        else:
            flag = jnp.float32(0.0)
        mk[2 + g, slot : slot + 1, :] = jnp.full((1, R), flag, F32)

    def start_own(u, carry):
        h, _, rows = part(u)
        cols = head_cols(g, h)
        for i, ref in enumerate((q_ref, do_ref)):
            pltpu.make_async_copy(ref.at[rows, cols], qd.at[2 + g, u, i], loc_s.at[0, u]).start()
        return carry

    def start_own_kv(h, carry):
        cols = head_cols(g, h)
        for i, ref in enumerate((k_ref, v_ref)):
            pltpu.make_async_copy(ref.at[:, cols], kv.at[h, g, i], loc_s.at[1, h]).start()
        return carry

    def send_part(k):
        u, i = k
        h, _, rows = part(u)
        ref = (do_ref, q_ref)[i]
        cols = head_cols(1 - g, h)
        remote(ref.at[rows, cols], qd.at[2 + g, u, 1 - i], send_s.at[0], qd_rs.at[2, u], mate).start()
        for side in range(2):

            @pl.when(present[side])
            def _():
                for core in range(2):
                    remote(
                        ref.at[rows, head_cols(core, h)], qd.at[slots[side], u, 1 - i], side_s.at[side, 0],
                        qd_rs.at[(3 + g, g)[side], u], chips[side][core],
                    ).start()

    def send_ahead(s, k):
        u = s + k // 2

        @pl.when(u < U)
        def _():
            send_part((u, k % 2))

    def send_kv(h):
        cols = head_cols(1 - g, h)
        for i, ref in enumerate((k_ref, v_ref)):
            remote(ref.at[:, cols], kv.at[h, g, i], send_s.at[1], kv_rs.at[h], mate).start()

    lax.fori_loop(0, HG, start_own_kv, 0)
    lax.fori_loop(0, U, start_own, 0)

    for side in range(2):

        @pl.when(jnp.logical_not(present[side]))
        def _():
            def clear(u, carry):
                for t in theirs_t[side]:
                    qd[t, u] = jnp.zeros((2, R, HD), BF16)
                row = lax.broadcasted_iota(jnp.int32, (8, R), 0)
                st_r[u, side] = jnp.where(lax.rem(row, 4) == 0, NEG, 0.0).astype(F32)
                ret_r[u, side] = jnp.zeros((8, R), F32)
                return carry

            lax.fori_loop(0, U, clear, 0)
            for t in theirs_t[side]:
                mk[t] = jnp.zeros((8, R), F32)
            dqr[side] = jnp.zeros((BLK, 2 * HG * HD), BF16)

    pl.semaphore_wait(barrier, 1 + 2 * sum(p_.astype(jnp.int32) for p_ in present))

    tile = mk.at[2 + g]
    remote(tile, tile, send_s.at[2], mk_rs.at[2], mate).start()
    for side in range(2):

        @pl.when(present[side])
        def _():
            for core in range(2):
                remote(
                    tile, mk.at[slots[side]], side_s.at[side, 1], mk_rs.at[(3 + g, g)[side]], chips[side][core]
                ).start()

    send_part((0, 0))
    send_part((0, 1))
    send_kv(0)
    for k in range(2, AHEAD):
        send_part((k // 2, k % 2))
    for h in range(1, HG):
        send_kv(h)

    def wait_side(u, side):
        @pl.when(present[side])
        def _():
            for i, t in enumerate(theirs_t[side]):
                wait_bytes(qd.at[t, u], qd_rs.at[3 * side + i, u])

    def first_pass(u, par):
        h = lax.div(u, SPLIT)

        def pair(j, carry):
            t, x = lax.div(j + 1, 2), lax.rem(j, 2)
            grads = nt(kv[h, x, 1], qd[t, u, 1])
            gw[par, j] = grads
            raw = nt(kv[h, x, 0], qd[t, u, 0])
            m = jnp.max(raw, axis=0, keepdims=True) * C2
            e = jnp.exp2(raw * C2 - m)
            p[par, j] = e
            mx[par, j, 0:1, :] = m
            mx[par, j, 1:2, :] = jnp.sum(e, axis=0, keepdims=True)
            mx[par, j, 2:3, :] = jnp.sum(e * grads, axis=0, keepdims=True)
            return carry

        return pair

    def attended(t, x):
        return mk[t, 4 - t + x : 5 - t + x, :] > 0.5

    def merge(entries):
        top = functools.reduce(jnp.maximum, [m for m, _, _ in entries])
        weights = [jnp.exp2(m - top) for m, _, _ in entries]
        total = sum(l * w for (_, l, _), w in zip(entries, weights))
        dots = sum(r * w for (_, _, r), w in zip(entries, weights))
        return top, total, dots

    def chip_stats(par, t):
        entries = []
        for x in range(2):
            if (t, x) in ((0, 1), (5, 0)):
                continue
            j = 2 * t - x
            on = attended(t, x)
            m = jnp.where(on, mx[par, j, 0:1, :], NEG)
            l = jnp.where(on, mx[par, j, 1:2, :], 0.0)
            r = jnp.where(on, mx[par, j, 2:3, :], 0.0)
            entries.append((m, l, r))
        return merge(entries)

    def send_stats(u, par, side):
        for i, t in enumerate(theirs_t[side]):
            for row, value in enumerate(chip_stats(par, t)):
                st_s[u, side, 4 * i + row : 4 * i + row + 1, :] = value

        @pl.when(present[side])
        def _():
            remote(
                st_s.at[u, side], st_r.at[u, 1 - side], side_s.at[side, 2], st_rs.at[1 - side, u], peers[side]
            ).start()

    def combine(u, par):
        for side in range(2):

            @pl.when(present[side])
            def _():
                wait_bytes(st_r.at[u, side], st_rs.at[side, u])

        for i, t in enumerate((2, 3)):
            entries = [chip_stats(par, t)]
            for side in range(2):
                entries.append(tuple(st_r[u, side, 4 * i + row : 4 * i + row + 1, :] for row in range(3)))
            top, total, dots = merge(entries)
            ret_s[u, 4 * i : 4 * i + 1, :] = top + jnp.log2(total)
            ret_s[u, 4 * i + 1 : 4 * i + 2, :] = dots / total
        for side in range(2):

            @pl.when(present[side])
            def _():
                remote(
                    ret_s.at[u], ret_r.at[u, 1 - side], side_s.at[side, 3], ret_rs.at[1 - side, u], peers[side]
                ).start()

    def factors(par, t, log_total, row_dot):
        for x in range(2):
            if (t, x) in ((0, 1), (5, 0)):
                continue
            j = 2 * t - x
            power = jnp.where(attended(t, x), mx[par, j, 0:1, :] - log_total, NEG)
            fr[j, 0:1, :] = jnp.exp2(power)
            fr[j, 1:2, :] = row_dot

    def second_pass(u, par):
        h = lax.div(u, SPLIT)

        def pair(j, carry):
            t, x = lax.div(j + 1, 2), lax.rem(j, 2)
            w = p[par, j] * fr[j, 0:1, :]
            low = w.astype(BF16)
            ds = (w * (gw[par, j] - fr[j, 1:2, :])).astype(BF16)
            acc[h, x, 1] += nn(low, qd[t, u, 1])
            acc[h, x, 0] += nn(ds, qd[t, u, 0])
            dqj[j] = tn(ds, kv[h, x, 0])
            return carry

        return pair

    def start_unit(u, par):
        h = lax.div(u, SPLIT)

        send_ahead(u, AHEAD)

        @pl.when(lax.rem(u, SPLIT) == 0)
        def _():
            wait_bytes(kv.at[h, g], loc_s.at[1, h])
            wait_bytes(kv.at[h, 1 - g], kv_rs.at[h])
            acc[h] = jnp.zeros((2, 2, BLK, HD), F32)

        @pl.when(u == 0)
        def _():
            wait_bytes(mk.at[3 - g], mk_rs.at[2])
            for side in range(2):

                @pl.when(present[side])
                def _():
                    for i, t in enumerate(theirs_t[side]):
                        wait_bytes(mk.at[t], mk_rs.at[3 * side + i])

        wait_bytes(qd.at[2 + g, u], loc_s.at[0, u])
        wait_bytes(qd.at[3 - g, u], qd_rs.at[2, u])
        pair = first_pass(u, par)
        lax.fori_loop(3, 7, pair, 0, unroll=True)
        wait_side(u, 0)
        lax.fori_loop(0, 3, pair, 0, unroll=True)
        send_stats(u, par, 0)
        wait_side(u, 1)
        lax.fori_loop(7, 10, pair, 0, unroll=True)
        send_stats(u, par, 1)
        send_ahead(u, AHEAD + 1)

    def finish_local(u, par):
        h, half, rows = part(u)
        cols = head_cols(g, h)
        for i, t in enumerate((2, 3)):
            factors(par, t, ret_s[u, 4 * i : 4 * i + 1, :], ret_s[u, 4 * i + 1 : 4 * i + 2, :])
        lax.fori_loop(3, 7, second_pass(u, par), 0, unroll=True)
        dqf[u, 0] = dqj[3] + dqj[4]
        dqf[u, 1] = dqj[5] + dqj[6]
        dq[rows, cols] = dqf[u, g]
        remote(dqf.at[u, 1 - g], dq.at[rows, cols], send_s.at[3], out_rs.at[2], mate).start()

        @pl.when(half == SPLIT - 1)
        def _():
            acc[h, :, 0] = acc[h, :, 0] * SCALE
            for i, out in enumerate((dk, dv)):
                out[:, cols] = acc[h, g, i]
                remote(acc.at[h, 1 - g, i], out.at[:, cols], send_s.at[4 + i], out_rs.at[3 + i], mate).start()

    def finish_remote(u, par):
        h, half, rows = part(u)
        cols = head_cols(g, h)
        pair = second_pass(u, par)

        for side, first in enumerate((0, 7)):

            @pl.when(present[side])
            def _():
                wait_bytes(ret_r.at[u, side], ret_rs.at[side, u])

            for i, t in enumerate(theirs_t[side]):
                factors(par, t, ret_r[u, side, 4 * i : 4 * i + 1, :], ret_r[u, side, 4 * i + 1 : 4 * i + 2, :])
            lax.fori_loop(first, first + 3, pair, 0, unroll=True)
            if side == 0:
                dqb[u, 0, 0] = dqj[0].astype(BF16)
                dqb[u, 0, 1] = (dqj[1] + dqj[2]).astype(BF16)
            else:
                dqb[u, 1, 0] = (dqj[7] + dqj[8]).astype(BF16)
                dqb[u, 1, 1] = dqj[9].astype(BF16)

            @pl.when(present[side])
            def _():
                for core in range(2):
                    remote(
                        dqb.at[u, side, core], dqr.at[1 - side, rows, cols], side_s.at[side, 4],
                        out_rs.at[1 - side], chips[side][core],
                    ).start()

    def step(s, carry):
        @pl.when(s < U)
        def _():
            start_unit(s, lax.rem(s, 2))

        @pl.when(s >= 1)
        def _():
            finish_remote(s - 1, lax.rem(s - 1, 2))
            finish_local(s - 1, lax.rem(s - 1, 2))

        @pl.when(s < U)
        def _():
            combine(s, lax.rem(s, 2))

        return carry

    lax.fori_loop(0, U + 1, step, 0)

    theirs = pl.ds(pl.multiple_of((1 - g) * HG * HD, HD), HG * HD)
    wait_bytes(qd.at[0], send_s.at[0])
    wait_bytes(kv.at[:, 0], send_s.at[1])
    wait_bytes(mk.at[0], send_s.at[2])
    wait_bytes(dqf.at[:, 0], send_s.at[3])
    wait_bytes(acc.at[:, 0, 0], send_s.at[4])
    wait_bytes(acc.at[:, 0, 1], send_s.at[5])
    wait_bytes(dk.at[:, theirs], out_rs.at[3])
    wait_bytes(dv.at[:, theirs], out_rs.at[4])
    wait_bytes(dq.at[:, theirs], out_rs.at[2])
    for side in range(2):

        @pl.when(present[side])
        def _():
            wait_bytes(qd.at[pl.ds(0, 2)], side_s.at[side, 0])
            wait_bytes(mk.at[pl.ds(0, 2)], side_s.at[side, 1])
            wait_bytes(st_s.at[:, 0], side_s.at[side, 2])
            wait_bytes(ret_s, side_s.at[side, 3])
            wait_bytes(dqb.at[:, 0], side_s.at[side, 4])
            wait_bytes(dqr.at[side], out_rs.at[side])

    def total(i, carry):
        rows = pl.ds(pl.multiple_of(i * 64, 64), 64)
        dq[rows, :] = (dq[rows, :] + dqr[0, rows, :].astype(F32) + dqr[1, rows, :].astype(F32)) * SCALE
        return carry

    lax.fori_loop(0, BLK // 64, total, 0, unroll=2)


def body(pb_size, kv_size, queries, keys, values, grad_out, offsets):
    rows, width = queries.shape
    any_space = pl.BlockSpec(memory_space=pl.ANY)
    vmem = pl.BlockSpec(memory_space=pltpu.VMEM)
    whole = jax.ShapeDtypeStruct((rows, width), F32)
    dma = pltpu.SemaphoreType.DMA
    in_hbm = [pltpu.with_memory_space_constraint(a, pltpu.HBM) for a in (queries, keys, values, grad_out, offsets)]
    grads = pl.pallas_call(
        functools.partial(kernel, pb_size, kv_size),
        out_shape=(whole,) * 3,
        in_specs=[any_space] * 5,
        out_specs=[vmem] * 3,
        scratch_shapes=[
            pltpu.VMEM((6, U, 2, R, HD), BF16),
            pltpu.VMEM((HG, 2, 2, BLK, HD), BF16),
            pltpu.VMEM((2, PAIRS, BLK, R), F32),
            pltpu.VMEM((2, PAIRS, BLK, R), F32),
            pltpu.VMEM((2, PAIRS, 8, R), F32),
            pltpu.VMEM((PAIRS, 8, R), F32),
            pltpu.VMEM((PAIRS, R, HD), F32),
            pltpu.VMEM((HG, 2, 2, BLK, HD), F32),
            pltpu.VMEM((U, 2, R, HD), F32),
            pltpu.VMEM((U, 2, 2, R, HD), BF16),
            pltpu.VMEM((2, BLK, 2 * HG * HD), BF16),
            pltpu.VMEM((U, 2, 8, R), F32),
            pltpu.VMEM((U, 2, 8, R), F32),
            pltpu.VMEM((U, 8, R), F32),
            pltpu.VMEM((U, 2, 8, R), F32),
            pltpu.VMEM((6, 8, R), F32),
            pltpu.SMEM((1, BAND), jnp.int32),
            dma((5, U)),
            dma((HG,)),
            dma((2, U)),
            dma((2, U)),
            dma((5,)),
            dma((5,)),
            dma((6,)),
            dma((2, 5)),
            dma((2, U)),
            dma((1,)),
        ],
        compiler_params=pltpu.CompilerParams(
            collective_id=0, has_side_effects=True, vmem_limit_bytes=VMEM_LIMIT
        ),
        cost_estimate=pl.CostEstimate(flops=14 * 10**9, bytes_accessed=16 << 20, transcendentals=10 * 2**20),
        name="band_backward",
    )(*in_hbm)
    return grads


def solution(mesh):
    spec = P(("pb", "kv"), None)
    return jax.shard_map(
        functools.partial(body, mesh.shape["pb"], mesh.shape["kv"]),
        mesh=mesh,
        in_specs=(spec,) * 5,
        out_specs=(spec,) * 3,
        check_vma=False,
    )
```

```python
import functools
import math

import jax
import jax.numpy as jnp
from jax import lax
from jax.experimental import pallas as pl
from jax.experimental.pallas import tpu as pltpu
from jax.sharding import PartitionSpec as P

HEADS = 8
BAND = 5
HG = HEADS // 2
HD = 128
BLK = 512
R = 256
SPLIT = BLK // R
U = HG * SPLIT
PAIRS = 10
DEPTH = 3
NEG = -1e30
SCALE = HD**-0.5
C2 = SCALE * math.log2(math.e)
MESH = pl.DeviceIdType.MESH
F32, BF16 = jnp.float32, jnp.bfloat16
AHEAD = 3
VMEM_LIMIT = 47 << 20


def nt(a, b):
    return lax.dot_general(a, b, (((1,), (1,)), ((), ())), preferred_element_type=F32)


def nn(a, b):
    return lax.dot_general(a, b, (((1,), (0,)), ((), ())), preferred_element_type=F32)


def tn(a, b):
    return lax.dot_general(a, b, (((0,), (0,)), ((), ())), preferred_element_type=F32)


def kernel(
    pb_size, kv_size,
    q_ref, k_ref, v_ref, do_ref, off_ref,
    dq, dk, dv,
    qd, kv, p, gw, mx, fr, dqj, acc, dqf, dqb, dqr, st_s, st_r, ret_s, ret_r, mk, off,
    qd_rs, kv_rs, st_rs, ret_rs, mk_rs, out_rs, send_s, side_s, loc_s, off_s,
):
    n = pb_size * kv_size
    me = lax.axis_index("pb") * kv_size + lax.axis_index("kv")
    g = lax.rem(me, 2)
    base = me - g

    def dev(block):
        block = lax.rem(block + n, n)
        return (lax.div(block, kv_size), lax.rem(block, kv_size))

    present = (base > 0, base + 2 < n)
    mate = dev(base + 1 - g)
    chips = ([dev(base - 2), dev(base - 1)], [dev(base + 2), dev(base + 3)])
    peers = (dev(me - 2), dev(me + 2))
    slots = (4 + g, g)
    theirs_t = ((0, 1), (4, 5))

    def remote(src, dst, send, recv, to):
        return pltpu.make_async_remote_copy(
            src_ref=src, dst_ref=dst, send_sem=send, recv_sem=recv, device_id=to, device_id_type=MESH
        )

    def wait_bytes(ref, sem):
        pltpu.make_async_copy(ref, ref, sem).wait()

    def part(u):
        h, half = lax.div(u, SPLIT), lax.rem(u, SPLIT)
        return h, half, pl.ds(pl.multiple_of(half * R, R), R)

    def head_cols(core, h):
        return pl.ds(pl.multiple_of((core * HG + h) * HD, HD), HD)

    barrier = pltpu.get_barrier_semaphore()
    pl.semaphore_signal(barrier, inc=1, device_id=mate, device_id_type=MESH)
    for side in range(2):

        @pl.when(present[side])
        def _():
            for to in chips[side]:
                pl.semaphore_signal(barrier, inc=1, device_id=to, device_id_type=MESH)

    copy = pltpu.make_async_copy(off_ref, off, off_s.at[0])
    copy.start()
    copy.wait()
    for slot in range(8):
        if slot < BAND:
            flag = jnp.where(off[0, slot] != 3, 1.0, 0.0).astype(F32)
        else:
            flag = jnp.float32(0.0)
        mk[2 + g, slot : slot + 1, :] = jnp.full((1, R), flag, F32)

    def start_own(u, carry):
        h, _, rows = part(u)
        cols = head_cols(g, h)
        for i, ref in enumerate((q_ref, do_ref)):
            pltpu.make_async_copy(ref.at[rows, cols], qd.at[2 + g, u, i], loc_s.at[0, u]).start()
        return carry

    def start_own_kv(h, carry):
        cols = head_cols(g, h)
        for i, ref in enumerate((k_ref, v_ref)):
            pltpu.make_async_copy(ref.at[:, cols], kv.at[h, g, i], loc_s.at[1, h]).start()
        return carry

    def send_part(k):
        u, i = k
        h, _, rows = part(u)
        ref = (do_ref, q_ref)[i]
        cols = head_cols(1 - g, h)
        remote(ref.at[rows, cols], qd.at[2 + g, u, 1 - i], send_s.at[0], qd_rs.at[2, u], mate).start()
        for side in range(2):

            @pl.when(present[side])
            def _():
                for core in range(2):
                    remote(
                        ref.at[rows, head_cols(core, h)], qd.at[slots[side], u, 1 - i], side_s.at[side, 0],
                        qd_rs.at[(3 + g, g)[side], u], chips[side][core],
                    ).start()

    def send_ahead(s, k):
        u = s + k // 2

        @pl.when(u < U)
        def _():
            send_part((u, k % 2))

    def send_kv(h):
        cols = head_cols(1 - g, h)
        for i, ref in enumerate((k_ref, v_ref)):
            remote(ref.at[:, cols], kv.at[h, g, i], send_s.at[1], kv_rs.at[h], mate).start()

    lax.fori_loop(0, HG, start_own_kv, 0)
    lax.fori_loop(0, U, start_own, 0)

    for side in range(2):

        @pl.when(jnp.logical_not(present[side]))
        def _():
            def clear(u, carry):
                for t in theirs_t[side]:
                    qd[t, u] = jnp.zeros((2, R, HD), BF16)
                row = lax.broadcasted_iota(jnp.int32, (8, R), 0)
                st_r[u, side] = jnp.where(lax.rem(row, 4) == 0, NEG, 0.0).astype(F32)
                ret_r[u, side] = jnp.zeros((8, R), F32)
                return carry

            lax.fori_loop(0, U, clear, 0)
            for t in theirs_t[side]:
                mk[t] = jnp.zeros((8, R), F32)
            dqr[side] = jnp.zeros((BLK, 2 * HG * HD), BF16)

    pl.semaphore_wait(barrier, 1 + 2 * sum(p_.astype(jnp.int32) for p_ in present))

    tile = mk.at[2 + g]
    remote(tile, tile, send_s.at[2], mk_rs.at[2], mate).start()
    for side in range(2):

        @pl.when(present[side])
        def _():
            for core in range(2):
                remote(
                    tile, mk.at[slots[side]], side_s.at[side, 1], mk_rs.at[(3 + g, g)[side]], chips[side][core]
                ).start()

    send_part((0, 0))
    send_part((0, 1))
    send_kv(0)
    for k in range(2, AHEAD):
        send_part((k // 2, k % 2))
    for h in range(1, HG):
        send_kv(h)

    def wait_side(u, side):
        @pl.when(present[side])
        def _():
            for i, t in enumerate(theirs_t[side]):
                wait_bytes(qd.at[t, u], qd_rs.at[3 * side + i, u])

    def first_pass(u, par):
        h = lax.div(u, SPLIT)

        def pair(j, carry):
            t, x = lax.div(j + 1, 2), lax.rem(j, 2)
            grads = nt(kv[h, x, 1], qd[t, u, 1])
            gw[par, j] = grads
            raw = nt(kv[h, x, 0], qd[t, u, 0])
            m = jnp.max(raw, axis=0, keepdims=True) * C2
            e = jnp.exp2(raw * C2 - m)
            p[par, j] = e
            mx[par, j, 0:1, :] = m
            mx[par, j, 1:2, :] = jnp.sum(e, axis=0, keepdims=True)
            mx[par, j, 2:3, :] = jnp.sum(e * grads, axis=0, keepdims=True)
            return carry

        return pair

    def attended(t, x):
        return mk[t, 4 - t + x : 5 - t + x, :] > 0.5

    def merge(entries):
        top = functools.reduce(jnp.maximum, [m for m, _, _ in entries])
        weights = [jnp.exp2(m - top) for m, _, _ in entries]
        total = sum(l * w for (_, l, _), w in zip(entries, weights))
        dots = sum(r * w for (_, _, r), w in zip(entries, weights))
        return top, total, dots

    def chip_stats(par, t):
        entries = []
        for x in range(2):
            if (t, x) in ((0, 1), (5, 0)):
                continue
            j = 2 * t - x
            on = attended(t, x)
            m = jnp.where(on, mx[par, j, 0:1, :], NEG)
            l = jnp.where(on, mx[par, j, 1:2, :], 0.0)
            r = jnp.where(on, mx[par, j, 2:3, :], 0.0)
            entries.append((m, l, r))
        return merge(entries)

    def send_stats(u, par, side):
        for i, t in enumerate(theirs_t[side]):
            for row, value in enumerate(chip_stats(par, t)):
                st_s[u, side, 4 * i + row : 4 * i + row + 1, :] = value

        @pl.when(present[side])
        def _():
            remote(
                st_s.at[u, side], st_r.at[u, 1 - side], side_s.at[side, 2], st_rs.at[1 - side, u], peers[side]
            ).start()

    def combine(u, par):
        for side in range(2):

            @pl.when(present[side])
            def _():
                wait_bytes(st_r.at[u, side], st_rs.at[side, u])

        for i, t in enumerate((2, 3)):
            entries = [chip_stats(par, t)]
            for side in range(2):
                entries.append(tuple(st_r[u, side, 4 * i + row : 4 * i + row + 1, :] for row in range(3)))
            top, total, dots = merge(entries)
            ret_s[u, 4 * i : 4 * i + 1, :] = top + jnp.log2(total)
            ret_s[u, 4 * i + 1 : 4 * i + 2, :] = dots / total
        for side in range(2):

            @pl.when(present[side])
            def _():
                remote(
                    ret_s.at[u], ret_r.at[u, 1 - side], side_s.at[side, 3], ret_rs.at[1 - side, u], peers[side]
                ).start()

    def factors(par, t, log_total, row_dot):
        for x in range(2):
            if (t, x) in ((0, 1), (5, 0)):
                continue
            j = 2 * t - x
            power = jnp.where(attended(t, x), mx[par, j, 0:1, :] - log_total, NEG)
            fr[j, 0:1, :] = jnp.exp2(power)
            fr[j, 1:2, :] = row_dot

    def second_pass(u, par, skip):
        h = lax.div(u, SPLIT)
        a = lax.rem(h, 2)

        def pair(j, carry):
            t, x = lax.div(j + 1, 2), lax.rem(j, 2)
            w = p[par, j] * fr[j, 0:1, :]
            low = w.astype(BF16)
            ds = (w * (gw[par, j] - fr[j, 1:2, :])).astype(BF16)
            acc[a, x, 1] += nn(low, qd[t, u, 1])
            acc[a, x, 0] += nn(ds, qd[t, u, 0])
            dqj[j - skip] = tn(ds, kv[h, x, 0])
            return carry

        return pair

    def start_unit(u, par):
        h = lax.div(u, SPLIT)

        send_ahead(u, AHEAD)

        @pl.when(lax.rem(u, SPLIT) == 0)
        def _():
            wait_bytes(kv.at[h, g], loc_s.at[1, h])
            wait_bytes(kv.at[h, 1 - g], kv_rs.at[h])

        @pl.when(u == 0)
        def _():
            wait_bytes(mk.at[3 - g], mk_rs.at[2])
            for side in range(2):

                @pl.when(present[side])
                def _():
                    for i, t in enumerate(theirs_t[side]):
                        wait_bytes(mk.at[t], mk_rs.at[3 * side + i])

        wait_bytes(qd.at[2 + g, u], loc_s.at[0, u])
        wait_bytes(qd.at[3 - g, u], qd_rs.at[2, u])
        pair = first_pass(u, par)
        lax.fori_loop(3, 7, pair, 0, unroll=True)
        wait_side(u, 0)
        lax.fori_loop(0, 3, pair, 0, unroll=True)
        send_stats(u, par, 0)
        wait_side(u, 1)
        lax.fori_loop(7, 10, pair, 0, unroll=True)
        send_stats(u, par, 1)
        send_ahead(u, AHEAD + 1)

    def finish_local(u, par):
        h, half, rows = part(u)
        cols = head_cols(g, h)
        for i, t in enumerate((2, 3)):
            factors(par, t, ret_s[u, 4 * i : 4 * i + 1, :], ret_s[u, 4 * i + 1 : 4 * i + 2, :])
        lax.fori_loop(3, 7, second_pass(u, par, 3), 0, unroll=True)
        dq[rows, cols] = dqj[2 * g] + dqj[2 * g + 1]
        slot = lax.rem(u, DEPTH)

        @pl.when(u >= DEPTH)
        def _():
            wait_bytes(dqf.at[0], send_s.at[8 + slot])

        dqf[slot] = dqj[2 - 2 * g] + dqj[3 - 2 * g]
        remote(dqf.at[slot], dq.at[rows, cols], send_s.at[8 + slot], out_rs.at[2], mate).start()

        @pl.when(half == SPLIT - 1)
        def _():
            a = lax.rem(h, 2)
            acc[a, :, 0] = acc[a, :, 0] * SCALE
            for i, out in enumerate((dk, dv)):
                out[:, cols] = acc[a, g, i]
                remote(
                    acc.at[a, 1 - g, i], out.at[:, cols], send_s.at[4 + 2 * a + i], out_rs.at[3 + i], mate
                ).start()

    def finish_remote(u, par):
        h, half, rows = part(u)
        cols = head_cols(g, h)
        slot = lax.rem(u, DEPTH)

        @pl.when(half == 0)
        def _():
            @pl.when(h >= 2)
            def _():
                for i in range(2):
                    wait_bytes(acc.at[0, 0, 0], send_s.at[4 + 2 * lax.rem(h, 2) + i])

            acc[lax.rem(h, 2)] = jnp.zeros((2, 2, BLK, HD), F32)

        for side, first in enumerate((0, 7)):

            @pl.when(present[side])
            def _():
                wait_bytes(ret_r.at[u, side], ret_rs.at[side, u])

            for i, t in enumerate(theirs_t[side]):
                factors(par, t, ret_r[u, side, 4 * i : 4 * i + 1, :], ret_r[u, side, 4 * i + 1 : 4 * i + 2, :])
            lax.fori_loop(first, first + 3, second_pass(u, par, 4 * side), 0, unroll=True)
            @pl.when(jnp.logical_and(present[side], u >= DEPTH))
            def _():
                wait_bytes(dqb.at[0, 0], side_s.at[side, 4 + slot])

            if side == 0:
                dqb[slot, 0, 0] = dqj[0].astype(BF16)
                dqb[slot, 0, 1] = (dqj[1] + dqj[2]).astype(BF16)
            else:
                dqb[slot, 1, 0] = (dqj[3] + dqj[4]).astype(BF16)
                dqb[slot, 1, 1] = dqj[5].astype(BF16)

            @pl.when(present[side])
            def _():
                for core in range(2):
                    remote(
                        dqb.at[slot, side, core], dqr.at[1 - side, rows, cols], side_s.at[side, 4 + slot],
                        out_rs.at[1 - side], chips[side][core],
                    ).start()

    def step(s, carry):
        @pl.when(s < U)
        def _():
            start_unit(s, lax.rem(s, DEPTH))

        @pl.when(jnp.logical_and(s >= 1, s < U + 1))
        def _():
            combine(s - 1, lax.rem(s - 1, DEPTH))

        @pl.when(s >= 2)
        def _():
            finish_remote(s - 2, lax.rem(s - 2, DEPTH))
            finish_local(s - 2, lax.rem(s - 2, DEPTH))

        return carry

    lax.fori_loop(0, U + 2, step, 0)

    theirs = pl.ds(pl.multiple_of((1 - g) * HG * HD, HD), HG * HD)
    wait_bytes(qd.at[0], send_s.at[0])
    wait_bytes(kv.at[:, 0], send_s.at[1])
    wait_bytes(mk.at[0], send_s.at[2])
    for slot in range(DEPTH):
        wait_bytes(dqf.at[0], send_s.at[8 + slot])
    for i in range(4):
        wait_bytes(acc.at[0, 0, 0], send_s.at[4 + i])
    wait_bytes(dk.at[:, theirs], out_rs.at[3])
    wait_bytes(dv.at[:, theirs], out_rs.at[4])
    wait_bytes(dq.at[:, theirs], out_rs.at[2])
    for side in range(2):

        @pl.when(present[side])
        def _():
            wait_bytes(qd.at[pl.ds(0, 2)], side_s.at[side, 0])
            wait_bytes(mk.at[pl.ds(0, 2)], side_s.at[side, 1])
            wait_bytes(st_s.at[:, 0], side_s.at[side, 2])
            wait_bytes(ret_s, side_s.at[side, 3])
            for slot in range(DEPTH):
                wait_bytes(dqb.at[0, 0], side_s.at[side, 4 + slot])
            wait_bytes(dqr.at[side], out_rs.at[side])

    def total(i, carry):
        rows = pl.ds(pl.multiple_of(i * 64, 64), 64)
        dq[rows, :] = (dq[rows, :] + dqr[0, rows, :].astype(F32) + dqr[1, rows, :].astype(F32)) * SCALE
        return carry

    lax.fori_loop(0, BLK // 64, total, 0, unroll=2)


def body(pb_size, kv_size, queries, keys, values, grad_out, offsets):
    rows, width = queries.shape
    any_space = pl.BlockSpec(memory_space=pl.ANY)
    vmem = pl.BlockSpec(memory_space=pltpu.VMEM)
    whole = jax.ShapeDtypeStruct((rows, width), F32)
    dma = pltpu.SemaphoreType.DMA
    in_hbm = [pltpu.with_memory_space_constraint(a, pltpu.HBM) for a in (queries, keys, values, grad_out, offsets)]
    grads = pl.pallas_call(
        functools.partial(kernel, pb_size, kv_size),
        out_shape=(whole,) * 3,
        in_specs=[any_space] * 5,
        out_specs=[vmem] * 3,
        scratch_shapes=[
            pltpu.VMEM((6, U, 2, R, HD), BF16),
            pltpu.VMEM((HG, 2, 2, BLK, HD), BF16),
            pltpu.VMEM((DEPTH, PAIRS, BLK, R), F32),
            pltpu.VMEM((DEPTH, PAIRS, BLK, R), F32),
            pltpu.VMEM((DEPTH, PAIRS, 8, R), F32),
            pltpu.VMEM((PAIRS, 8, R), F32),
            pltpu.VMEM((6, R, HD), F32),
            pltpu.VMEM((2, 2, 2, BLK, HD), F32),
            pltpu.VMEM((DEPTH, R, HD), F32),
            pltpu.VMEM((DEPTH, 2, 2, R, HD), BF16),
            pltpu.VMEM((2, BLK, 2 * HG * HD), BF16),
            pltpu.VMEM((U, 2, 8, R), F32),
            pltpu.VMEM((U, 2, 8, R), F32),
            pltpu.VMEM((U, 8, R), F32),
            pltpu.VMEM((U, 2, 8, R), F32),
            pltpu.VMEM((6, 8, R), F32),
            pltpu.SMEM((1, BAND), jnp.int32),
            dma((5, U)),
            dma((HG,)),
            dma((2, U)),
            dma((2, U)),
            dma((5,)),
            dma((5,)),
            dma((8 + DEPTH,)),
            dma((2, 4 + DEPTH)),
            dma((2, U)),
            dma((1,)),
        ],
        compiler_params=pltpu.CompilerParams(
            collective_id=0, has_side_effects=True, vmem_limit_bytes=VMEM_LIMIT
        ),
        cost_estimate=pl.CostEstimate(flops=14 * 10**9, bytes_accessed=16 << 20, transcendentals=10 * 2**20),
        name="band_backward",
    )(*in_hbm)
    return grads


def solution(mesh):
    spec = P(("pb", "kv"), None)
    return jax.shard_map(
        functools.partial(body, mesh.shape["pb"], mesh.shape["kv"]),
        mesh=mesh,
        in_specs=(spec,) * 5,
        out_specs=(spec,) * 3,
        check_vma=False,
    )
```

```python
import functools
import math

import jax
import jax.numpy as jnp
from jax import lax
from jax.experimental import pallas as pl
from jax.experimental.pallas import tpu as pltpu
from jax.sharding import PartitionSpec as P

HEADS = 8
BAND = 5
HG = HEADS // 2
HD = 128
BLK = 512
R = 256
SPLIT = BLK // R
U = HG * SPLIT
PAIRS = 10
DEPTH = 3
NEG = -1e30
SCALE = HD**-0.5
C2 = SCALE * math.log2(math.e)
MESH = pl.DeviceIdType.MESH
F32, BF16 = jnp.float32, jnp.bfloat16
AHEAD = 3
VMEM_LIMIT = 47 << 20


def nt(a, b):
    return lax.dot_general(a, b, (((1,), (1,)), ((), ())), preferred_element_type=F32)


def nn(a, b):
    return lax.dot_general(a, b, (((1,), (0,)), ((), ())), preferred_element_type=F32)


def tn(a, b):
    return lax.dot_general(a, b, (((0,), (0,)), ((), ())), preferred_element_type=F32)


def kernel(
    pb_size, kv_size,
    q_ref, k_ref, v_ref, do_ref, off_ref,
    dq, dk, dv,
    qd, kv, p, gw, mx, fr, dqj, acc, dqf, dqb, dqr, st_s, st_r, ret_s, ret_r, mk, off,
    qd_rs, kv_rs, st_rs, ret_rs, mk_rs, out_rs, dq_rs, send_s, side_s, loc_s, off_s,
):
    n = pb_size * kv_size
    me = lax.axis_index("pb") * kv_size + lax.axis_index("kv")
    g = lax.rem(me, 2)
    base = me - g

    def dev(block):
        block = lax.rem(block + n, n)
        return (lax.div(block, kv_size), lax.rem(block, kv_size))

    present = (base > 0, base + 2 < n)
    mate = dev(base + 1 - g)
    chips = ([dev(base - 2), dev(base - 1)], [dev(base + 2), dev(base + 3)])
    peers = (dev(me - 2), dev(me + 2))
    slots = (4 + g, g)
    theirs_t = ((0, 1), (4, 5))

    def remote(src, dst, send, recv, to):
        return pltpu.make_async_remote_copy(
            src_ref=src, dst_ref=dst, send_sem=send, recv_sem=recv, device_id=to, device_id_type=MESH
        )

    def wait_bytes(ref, sem):
        pltpu.make_async_copy(ref, ref, sem).wait()

    def part(u):
        h, half = lax.div(u, SPLIT), lax.rem(u, SPLIT)
        return h, half, pl.ds(pl.multiple_of(half * R, R), R)

    def head_cols(core, h):
        return pl.ds(pl.multiple_of((core * HG + h) * HD, HD), HD)

    barrier = pltpu.get_barrier_semaphore()
    pl.semaphore_signal(barrier, inc=1, device_id=mate, device_id_type=MESH)
    for side in range(2):

        @pl.when(present[side])
        def _():
            for to in chips[side]:
                pl.semaphore_signal(barrier, inc=1, device_id=to, device_id_type=MESH)

    copy = pltpu.make_async_copy(off_ref, off, off_s.at[0])
    copy.start()
    copy.wait()
    for slot in range(8):
        if slot < BAND:
            flag = jnp.where(off[0, slot] != 3, 1.0, 0.0).astype(F32)
        else:
            flag = jnp.float32(0.0)
        mk[2 + g, slot : slot + 1, :] = jnp.full((1, R), flag, F32)

    def start_own(u, carry):
        h, _, rows = part(u)
        cols = head_cols(g, h)
        for i, ref in enumerate((q_ref, do_ref)):
            pltpu.make_async_copy(ref.at[rows, cols], qd.at[2 + g, u, i], loc_s.at[0, u]).start()
        return carry

    def start_own_kv(h, carry):
        cols = head_cols(g, h)
        for i, ref in enumerate((k_ref, v_ref)):
            pltpu.make_async_copy(ref.at[:, cols], kv.at[h, g, i], loc_s.at[1, h]).start()
        return carry

    def send_part(k):
        u, i = k
        h, _, rows = part(u)
        ref = (do_ref, q_ref)[i]
        cols = head_cols(1 - g, h)
        remote(ref.at[rows, cols], qd.at[2 + g, u, 1 - i], send_s.at[0], qd_rs.at[2, u], mate).start()
        for side in range(2):

            @pl.when(present[side])
            def _():
                for core in range(2):
                    remote(
                        ref.at[rows, head_cols(core, h)], qd.at[slots[side], u, 1 - i], side_s.at[side, 0],
                        qd_rs.at[(3 + g, g)[side], u], chips[side][core],
                    ).start()

    def send_ahead(s, k):
        u = s + k // 2

        @pl.when(u < U)
        def _():
            send_part((u, k % 2))

    def send_kv(h):
        cols = head_cols(1 - g, h)
        for i, ref in enumerate((k_ref, v_ref)):
            remote(ref.at[:, cols], kv.at[h, g, i], send_s.at[1], kv_rs.at[h], mate).start()

    lax.fori_loop(0, HG, start_own_kv, 0)
    lax.fori_loop(0, U, start_own, 0)

    for side in range(2):

        @pl.when(jnp.logical_not(present[side]))
        def _():
            def clear(u, carry):
                for t in theirs_t[side]:
                    qd[t, u] = jnp.zeros((2, R, HD), BF16)
                for row in range(4):
                    st_r[u, side, row : row + 1, :] = jnp.full((1, R), 0.0 if row % 2 else NEG, F32)
                ret_r[u, side] = jnp.zeros((4, R), F32)
                return carry

            lax.fori_loop(0, U, clear, 0)
            for t in theirs_t[side]:
                mk[t] = jnp.zeros((8, R), F32)
            dqr[side] = jnp.zeros((BLK, 2 * HG * HD), BF16)

    pl.semaphore_wait(barrier, 1 + 2 * sum(p_.astype(jnp.int32) for p_ in present))

    tile = mk.at[2 + g]
    remote(tile, tile, send_s.at[2], mk_rs.at[2], mate).start()
    for side in range(2):

        @pl.when(present[side])
        def _():
            for core in range(2):
                remote(
                    tile, mk.at[slots[side]], side_s.at[side, 1], mk_rs.at[(3 + g, g)[side]], chips[side][core]
                ).start()

    send_part((0, 0))
    send_part((0, 1))
    send_kv(0)
    for k in range(2, AHEAD):
        send_part((k // 2, k % 2))
    for h in range(1, HG):
        send_kv(h)

    def wait_side(u, side):
        @pl.when(present[side])
        def _():
            for i, t in enumerate(theirs_t[side]):
                wait_bytes(qd.at[t, u], qd_rs.at[3 * side + i, u])

    def first_pass(u, par):
        h = lax.div(u, SPLIT)

        def pair(j, carry):
            t, x = lax.div(j + 1, 2), lax.rem(j, 2)
            grads = nt(kv[h, x, 1], qd[t, u, 1])
            gw[par, j] = grads
            raw = nt(kv[h, x, 0], qd[t, u, 0])
            m = jnp.max(raw, axis=0, keepdims=True) * C2
            e = jnp.exp2(raw * C2 - m)
            p[par, j] = e
            mx[par, j, 0:1, :] = m
            mx[par, j, 1:2, :] = jnp.sum(e, axis=0, keepdims=True)
            mx[par, j, 2:3, :] = jnp.sum(e * grads, axis=0, keepdims=True)
            return carry

        return pair

    def attended(t, x):
        return mk[t, 4 - t + x : 5 - t + x, :] > 0.5

    def merge(entries):
        top = functools.reduce(jnp.maximum, [a for a, _ in entries])
        weights = [jnp.exp2(a - top) for a, _ in entries]
        total = sum(weights)
        return top + jnp.log2(total), sum(b * w for (_, b), w in zip(entries, weights)) / total

    def chip_stats(par, t):
        entries = []
        for x in range(2):
            if (t, x) in ((0, 1), (5, 0)):
                continue
            j = 2 * t - x
            on = attended(t, x)
            total = mx[par, j, 1:2, :]
            log_part = mx[par, j, 0:1, :] + jnp.log2(total)
            entries.append((jnp.where(on, log_part, NEG), jnp.where(on, mx[par, j, 2:3, :] / total, 0.0)))
        return entries

    def send_stats(u, par, side):
        for i, t in enumerate(theirs_t[side]):
            for row, value in enumerate(merge(chip_stats(par, t))):
                st_s[u, side, 2 * i + row : 2 * i + row + 1, :] = value

        @pl.when(present[side])
        def _():
            remote(
                st_s.at[u, side], st_r.at[u, 1 - side], side_s.at[side, 2], st_rs.at[1 - side, u], peers[side]
            ).start()

    def combine(u, par):
        for side in range(2):

            @pl.when(present[side])
            def _():
                wait_bytes(st_r.at[u, side], st_rs.at[side, u])

        for i, t in enumerate((2, 3)):
            entries = chip_stats(par, t)
            for side in range(2):
                entries.append(tuple(st_r[u, side, 2 * i + row : 2 * i + row + 1, :] for row in range(2)))
            for row, value in enumerate(merge(entries)):
                ret_s[u, 2 * i + row : 2 * i + row + 1, :] = value
        for side in range(2):

            @pl.when(present[side])
            def _():
                remote(
                    ret_s.at[u], ret_r.at[u, 1 - side], side_s.at[side, 3], ret_rs.at[1 - side, u], peers[side]
                ).start()

    def factors(par, t, log_total, row_dot):
        for x in range(2):
            if (t, x) in ((0, 1), (5, 0)):
                continue
            j = 2 * t - x
            power = jnp.where(attended(t, x), mx[par, j, 0:1, :] - log_total, NEG)
            fr[j, 0:1, :] = jnp.exp2(power)
            fr[j, 1:2, :] = row_dot

    def second_pass(u, par, skip):
        h = lax.div(u, SPLIT)
        a = lax.rem(h, 2)

        def pair(j, carry):
            t, x = lax.div(j + 1, 2), lax.rem(j, 2)
            w = p[par, j] * fr[j, 0:1, :]
            low = w.astype(BF16)
            ds = (w * (gw[par, j] - fr[j, 1:2, :])).astype(BF16)
            acc[a, x, 1] += nn(low, qd[t, u, 1])
            acc[a, x, 0] += nn(ds, qd[t, u, 0])
            dqj[j - skip] = tn(ds, kv[h, x, 0])
            return carry

        return pair

    def start_unit(u, par):
        h = lax.div(u, SPLIT)

        send_ahead(u, AHEAD)

        @pl.when(lax.rem(u, SPLIT) == 0)
        def _():
            wait_bytes(kv.at[h, g], loc_s.at[1, h])
            wait_bytes(kv.at[h, 1 - g], kv_rs.at[h])

        @pl.when(u == 0)
        def _():
            wait_bytes(mk.at[3 - g], mk_rs.at[2])
            for side in range(2):

                @pl.when(present[side])
                def _():
                    for i, t in enumerate(theirs_t[side]):
                        wait_bytes(mk.at[t], mk_rs.at[3 * side + i])

        wait_bytes(qd.at[2 + g, u], loc_s.at[0, u])
        wait_bytes(qd.at[3 - g, u], qd_rs.at[2, u])
        pair = first_pass(u, par)
        lax.fori_loop(3, 7, pair, 0, unroll=True)
        wait_side(u, 0)
        lax.fori_loop(0, 3, pair, 0, unroll=True)
        send_stats(u, par, 0)
        wait_side(u, 1)
        lax.fori_loop(7, 10, pair, 0, unroll=True)
        send_stats(u, par, 1)
        send_ahead(u, AHEAD + 1)

    def finish_local(u, par):
        h, half, rows = part(u)
        cols = head_cols(g, h)
        for i, t in enumerate((2, 3)):
            factors(par, t, ret_s[u, 2 * i : 2 * i + 1, :], ret_s[u, 2 * i + 1 : 2 * i + 2, :])
        lax.fori_loop(3, 7, second_pass(u, par, 3), 0, unroll=True)
        dq[rows, cols] = dqj[2 * g] + dqj[2 * g + 1]
        slot = lax.rem(u, DEPTH)

        @pl.when(u >= DEPTH)
        def _():
            wait_bytes(dqf.at[0], send_s.at[8 + slot])

        dqf[slot] = dqj[2 - 2 * g] + dqj[3 - 2 * g]
        remote(dqf.at[slot], dq.at[rows, cols], send_s.at[8 + slot], dq_rs.at[2, h], mate).start()

        @pl.when(half == SPLIT - 1)
        def _():
            a = lax.rem(h, 2)
            acc[a, :, 0] = acc[a, :, 0] * SCALE
            for i, out in enumerate((dk, dv)):
                out[:, cols] = acc[a, g, i]
                remote(
                    acc.at[a, 1 - g, i], out.at[:, cols], send_s.at[4 + 2 * a + i], out_rs.at[i], mate
                ).start()

    def open_head(u):
        h, half, _ = part(u)

        @pl.when(half == 0)
        def _():
            @pl.when(h >= 2)
            def _():
                for i in range(2):
                    wait_bytes(acc.at[0, 0, 0], send_s.at[4 + 2 * lax.rem(h, 2) + i])

            acc[lax.rem(h, 2)] = jnp.zeros((2, 2, BLK, HD), F32)

    def finish_remote(u, par):
        h, half, rows = part(u)
        cols = head_cols(g, h)
        slot = lax.rem(u, DEPTH)

        for side, first in enumerate((0, 7)):

            @pl.when(present[side])
            def _():
                wait_bytes(ret_r.at[u, side], ret_rs.at[side, u])

            for i, t in enumerate(theirs_t[side]):
                factors(par, t, ret_r[u, side, 2 * i : 2 * i + 1, :], ret_r[u, side, 2 * i + 1 : 2 * i + 2, :])
            lax.fori_loop(first, first + 3, second_pass(u, par, 4 * side), 0, unroll=True)
            @pl.when(jnp.logical_and(present[side], u >= DEPTH))
            def _():
                wait_bytes(dqb.at[0, 0], side_s.at[side, 4 + slot])

            if side == 0:
                dqb[slot, 0, 0] = dqj[0].astype(BF16)
                dqb[slot, 0, 1] = (dqj[1] + dqj[2]).astype(BF16)
            else:
                dqb[slot, 1, 0] = (dqj[3] + dqj[4]).astype(BF16)
                dqb[slot, 1, 1] = dqj[5].astype(BF16)

            @pl.when(present[side])
            def _():
                for core in range(2):
                    remote(
                        dqb.at[slot, side, core], dqr.at[1 - side, rows, cols], side_s.at[side, 4 + slot],
                        dq_rs.at[1 - side, h], chips[side][core],
                    ).start()

    def step(s, carry):
        @pl.when(s < U)
        def _():
            start_unit(s, lax.rem(s, DEPTH))

        @pl.when(s >= 2)
        def _():
            open_head(s - 2)

        @pl.when(s == U)
        def _():
            finish_local(s - 2, lax.rem(s - 2, DEPTH))

        @pl.when(jnp.logical_and(s >= 1, s < U + 1))
        def _():
            combine(s - 1, lax.rem(s - 1, DEPTH))

        @pl.when(s >= 2)
        def _():
            finish_remote(s - 2, lax.rem(s - 2, DEPTH))

        @pl.when(jnp.logical_and(s >= 2, s != U))
        def _():
            finish_local(s - 2, lax.rem(s - 2, DEPTH))

        return carry

    lax.fori_loop(0, U + 2, step, 0)

    theirs = pl.ds(pl.multiple_of((1 - g) * HG * HD, HD), HG * HD)
    for h in range(HG):
        for side in range(2):

            @pl.when(present[side])
            def _():
                wait_bytes(dqr.at[side, :, pl.ds(0, 2 * HD)], dq_rs.at[side, h])

        wait_bytes(dq.at[:, pl.ds(0, HD)], dq_rs.at[2, h])
        for core in range(2):
            cols = head_cols(core, h)

            def total(i, carry):
                rows = pl.ds(pl.multiple_of(i * 128, 128), 128)
                dq[rows, cols] = (
                    dq[rows, cols] + dqr[0, rows, cols].astype(F32) + dqr[1, rows, cols].astype(F32)
                ) * SCALE
                return carry

            lax.fori_loop(0, BLK // 128, total, 0, unroll=2)
    wait_bytes(qd.at[0], send_s.at[0])
    wait_bytes(kv.at[:, 0], send_s.at[1])
    wait_bytes(mk.at[0], send_s.at[2])
    for slot in range(DEPTH):
        wait_bytes(dqf.at[0], send_s.at[8 + slot])
    for i in range(4):
        wait_bytes(acc.at[0, 0, 0], send_s.at[4 + i])
    for side in range(2):

        @pl.when(present[side])
        def _():
            wait_bytes(qd.at[pl.ds(0, 2)], side_s.at[side, 0])
            wait_bytes(mk.at[pl.ds(0, 2)], side_s.at[side, 1])
            wait_bytes(st_s.at[:, 0], side_s.at[side, 2])
            wait_bytes(ret_s, side_s.at[side, 3])
            for slot in range(DEPTH):
                wait_bytes(dqb.at[0, 0], side_s.at[side, 4 + slot])

    wait_bytes(dk.at[:, theirs], out_rs.at[0])
    wait_bytes(dv.at[:, theirs], out_rs.at[1])


def write_out(dq, dk, dv, dq_out, dk_out, dv_out, sems):
    copies = [
        pltpu.make_async_copy(src, dst, sems.at[i])
        for i, (src, dst) in enumerate(((dq, dq_out), (dk, dk_out), (dv, dv_out)))
    ]
    for copy in copies:
        copy.start()
    for copy in copies:
        copy.wait()


def body(pb_size, kv_size, queries, keys, values, grad_out, offsets):
    rows, width = queries.shape
    any_space = pl.BlockSpec(memory_space=pl.ANY)
    vmem = pl.BlockSpec(memory_space=pltpu.VMEM)
    whole = jax.ShapeDtypeStruct((rows, width), F32)
    dma = pltpu.SemaphoreType.DMA
    in_hbm = [pltpu.with_memory_space_constraint(a, pltpu.HBM) for a in (queries, keys, values, grad_out, offsets)]
    grads = pl.pallas_call(
        functools.partial(kernel, pb_size, kv_size),
        out_shape=(whole,) * 3,
        in_specs=[any_space] * 5,
        out_specs=[vmem] * 3,
        scratch_shapes=[
            pltpu.VMEM((6, U, 2, R, HD), BF16),
            pltpu.VMEM((HG, 2, 2, BLK, HD), BF16),
            pltpu.VMEM((DEPTH, PAIRS, BLK, R), F32),
            pltpu.VMEM((DEPTH, PAIRS, BLK, R), F32),
            pltpu.VMEM((DEPTH, PAIRS, 8, R), F32),
            pltpu.VMEM((PAIRS, 8, R), F32),
            pltpu.VMEM((6, R, HD), F32),
            pltpu.VMEM((2, 2, 2, BLK, HD), F32),
            pltpu.VMEM((DEPTH, R, HD), F32),
            pltpu.VMEM((DEPTH, 2, 2, R, HD), BF16),
            pltpu.VMEM((2, BLK, 2 * HG * HD), BF16),
            pltpu.VMEM((U, 2, 4, R), F32),
            pltpu.VMEM((U, 2, 4, R), F32),
            pltpu.VMEM((U, 4, R), F32),
            pltpu.VMEM((U, 2, 4, R), F32),
            pltpu.VMEM((6, 8, R), F32),
            pltpu.SMEM((1, BAND), jnp.int32),
            dma((5, U)),
            dma((HG,)),
            dma((2, U)),
            dma((2, U)),
            dma((5,)),
            dma((2,)),
            dma((3, HG)),
            dma((8 + DEPTH,)),
            dma((2, 4 + DEPTH)),
            dma((2, U)),
            dma((1,)),
        ],
        compiler_params=pltpu.CompilerParams(
            collective_id=0, has_side_effects=True, vmem_limit_bytes=VMEM_LIMIT
        ),
        cost_estimate=pl.CostEstimate(flops=14 * 10**9, bytes_accessed=16 << 20, transcendentals=10 * 2**20),
        name="band_backward",
    )(*in_hbm)
    in_vmem = [pltpu.with_memory_space_constraint(a, pltpu.VMEM) for a in grads]
    return pl.pallas_call(
        write_out,
        out_shape=(whole,) * 3,
        in_specs=[any_space] * 3,
        out_specs=[any_space] * 3,
        scratch_shapes=[dma((3,))],
        compiler_params=pltpu.CompilerParams(vmem_limit_bytes=1 << 20),
        name="write_out",
    )(*in_vmem)


def solution(mesh):
    spec = P(("pb", "kv"), None)
    return jax.shard_map(
        functools.partial(body, mesh.shape["pb"], mesh.shape["kv"]),
        mesh=mesh,
        in_specs=(spec,) * 5,
        out_specs=(spec,) * 3,
        check_vma=False,
    )
```

```python
import functools
import math

import jax
import jax.numpy as jnp
from jax import lax
from jax.experimental import pallas as pl
from jax.experimental.pallas import tpu as pltpu
from jax.sharding import PartitionSpec as P

HEADS = 8
BAND = 5
HG = HEADS // 2
HD = 128
BLK = 512
R = 256
SPLIT = BLK // R
U = HG * SPLIT
PAIRS = 10
DEPTH = 3
NEG = -1e30
SCALE = HD**-0.5
C2 = SCALE * math.log2(math.e)
MESH = pl.DeviceIdType.MESH
F32, BF16 = jnp.float32, jnp.bfloat16
AHEAD = 4
VMEM_LIMIT = 47 << 20


def nt(a, b):
    return lax.dot_general(a, b, (((1,), (1,)), ((), ())), preferred_element_type=F32)


def nn(a, b):
    return lax.dot_general(a, b, (((1,), (0,)), ((), ())), preferred_element_type=F32)


def tn(a, b):
    return lax.dot_general(a, b, (((0,), (0,)), ((), ())), preferred_element_type=F32)


def kernel(
    pb_size, kv_size,
    q_ref, k_ref, v_ref, do_ref, off_ref,
    dq, dk, dv,
    qd, kv, p, gw, mx, fr, dqj, acc, dqf, dqb, dqr, st_s, st_r, ret_s, ret_r, mk, off,
    qd_rs, kv_rs, st_rs, ret_rs, mk_rs, out_rs, dq_rs, send_s, side_s, loc_s, off_s,
):
    n = pb_size * kv_size
    me = lax.axis_index("pb") * kv_size + lax.axis_index("kv")
    g = lax.rem(me, 2)
    base = me - g

    def dev(block):
        block = lax.rem(block + n, n)
        return (lax.div(block, kv_size), lax.rem(block, kv_size))

    present = (base > 0, base + 2 < n)
    mate = dev(base + 1 - g)
    chips = ([dev(base - 2), dev(base - 1)], [dev(base + 2), dev(base + 3)])
    peers = (dev(me - 2), dev(me + 2))
    slots = (4 + g, g)
    theirs_t = ((0, 1), (4, 5))

    def remote(src, dst, send, recv, to):
        return pltpu.make_async_remote_copy(
            src_ref=src, dst_ref=dst, send_sem=send, recv_sem=recv, device_id=to, device_id_type=MESH
        )

    def wait_bytes(ref, sem):
        pltpu.make_async_copy(ref, ref, sem).wait()

    def part(u):
        h, half = lax.div(u, SPLIT), lax.rem(u, SPLIT)
        return h, half, pl.ds(pl.multiple_of(half * R, R), R)

    def head_cols(core, h):
        return pl.ds(pl.multiple_of((core * HG + h) * HD, HD), HD)

    barrier = pltpu.get_barrier_semaphore()
    pl.semaphore_signal(barrier, inc=1, device_id=mate, device_id_type=MESH)
    for side in range(2):

        @pl.when(present[side])
        def _():
            for to in chips[side]:
                pl.semaphore_signal(barrier, inc=1, device_id=to, device_id_type=MESH)

    copy = pltpu.make_async_copy(off_ref, off, off_s.at[0])
    copy.start()
    copy.wait()
    for slot in range(8):
        if slot < BAND:
            flag = jnp.where(off[0, slot] != 3, 1.0, 0.0).astype(F32)
        else:
            flag = jnp.float32(0.0)
        mk[2 + g, slot : slot + 1, :] = jnp.full((1, R), flag, F32)

    def start_own(u, carry):
        h, _, rows = part(u)
        cols = head_cols(g, h)
        for i, ref in enumerate((q_ref, do_ref)):
            pltpu.make_async_copy(ref.at[rows, cols], qd.at[2 + g, u, i], loc_s.at[0, u]).start()
        return carry

    def start_own_kv(h, carry):
        cols = head_cols(g, h)
        for i, ref in enumerate((k_ref, v_ref)):
            pltpu.make_async_copy(ref.at[:, cols], kv.at[h, g, i], loc_s.at[1, h]).start()
        return carry

    def send_part(k):
        u, i = k
        h, _, rows = part(u)
        ref = (do_ref, q_ref)[i]
        cols = head_cols(1 - g, h)
        remote(ref.at[rows, cols], qd.at[2 + g, u, 1 - i], send_s.at[0], qd_rs.at[2, u], mate).start()
        for side in range(2):

            @pl.when(present[side])
            def _():
                for core in range(2):
                    remote(
                        ref.at[rows, head_cols(core, h)], qd.at[slots[side], u, 1 - i], side_s.at[side, 0],
                        qd_rs.at[(3 + g, g)[side], u], chips[side][core],
                    ).start()

    def send_ahead(s, k):
        u = s + k // 2

        @pl.when(u < U)
        def _():
            send_part((u, k % 2))

    def send_kv(h):
        cols = head_cols(1 - g, h)
        for i, ref in enumerate((k_ref, v_ref)):
            remote(ref.at[:, cols], kv.at[h, g, i], send_s.at[1], kv_rs.at[h], mate).start()

    lax.fori_loop(0, HG, start_own_kv, 0)
    lax.fori_loop(0, U, start_own, 0)

    for side in range(2):

        @pl.when(jnp.logical_not(present[side]))
        def _():
            def clear(u, carry):
                for t in theirs_t[side]:
                    qd[t, u] = jnp.zeros((2, R, HD), BF16)
                for row in range(4):
                    st_r[u, side, row : row + 1, :] = jnp.full((1, R), 0.0 if row % 2 else NEG, F32)
                ret_r[u, side] = jnp.zeros((4, R), F32)
                return carry

            lax.fori_loop(0, U, clear, 0)
            for t in theirs_t[side]:
                mk[t] = jnp.zeros((8, R), F32)
            dqr[side] = jnp.zeros((BLK, 2 * HG * HD), BF16)

    pl.semaphore_wait(barrier, 1 + 2 * sum(p_.astype(jnp.int32) for p_ in present))

    tile = mk.at[2 + g]
    remote(tile, tile, send_s.at[2], mk_rs.at[2], mate).start()
    for side in range(2):

        @pl.when(present[side])
        def _():
            for core in range(2):
                remote(
                    tile, mk.at[slots[side]], side_s.at[side, 1], mk_rs.at[(3 + g, g)[side]], chips[side][core]
                ).start()

    send_part((0, 0))
    send_part((0, 1))
    send_kv(0)
    for k in range(2, AHEAD):
        send_part((k // 2, k % 2))
    for h in range(1, HG):
        send_kv(h)

    def wait_side(u, side):
        @pl.when(present[side])
        def _():
            for i, t in enumerate(theirs_t[side]):
                wait_bytes(qd.at[t, u], qd_rs.at[3 * side + i, u])

    def first_pass(u, par):
        h = lax.div(u, SPLIT)

        def pair(j, carry):
            t, x = lax.div(j + 1, 2), lax.rem(j, 2)
            grads = nt(kv[h, x, 1], qd[t, u, 1])
            gw[par, j] = grads
            raw = nt(kv[h, x, 0], qd[t, u, 0])
            m = jnp.max(raw, axis=0, keepdims=True) * C2
            e = jnp.exp2(raw * C2 - m)
            p[par, j] = e
            mx[par, j, 0:1, :] = m
            mx[par, j, 1:2, :] = jnp.sum(e, axis=0, keepdims=True)
            mx[par, j, 2:3, :] = jnp.sum(e * grads, axis=0, keepdims=True)
            return carry

        return pair

    def attended(t, x):
        return mk[t, 4 - t + x : 5 - t + x, :] > 0.5

    def merge(entries):
        top = functools.reduce(jnp.maximum, [a for a, _ in entries])
        weights = [jnp.exp2(a - top) for a, _ in entries]
        total = sum(weights)
        return top + jnp.log2(total), sum(b * w for (_, b), w in zip(entries, weights)) / total

    def chip_stats(par, t):
        entries = []
        for x in range(2):
            if (t, x) in ((0, 1), (5, 0)):
                continue
            j = 2 * t - x
            on = attended(t, x)
            total = mx[par, j, 1:2, :]
            log_part = mx[par, j, 0:1, :] + jnp.log2(total)
            entries.append((jnp.where(on, log_part, NEG), jnp.where(on, mx[par, j, 2:3, :] / total, 0.0)))
        return entries

    def send_stats(u, par, side):
        for i, t in enumerate(theirs_t[side]):
            for row, value in enumerate(merge(chip_stats(par, t))):
                st_s[u, side, 2 * i + row : 2 * i + row + 1, :] = value

        @pl.when(present[side])
        def _():
            remote(
                st_s.at[u, side], st_r.at[u, 1 - side], side_s.at[side, 2], st_rs.at[1 - side, u], peers[side]
            ).start()

    def combine(u, par):
        for side in range(2):

            @pl.when(present[side])
            def _():
                wait_bytes(st_r.at[u, side], st_rs.at[side, u])

        for i, t in enumerate((2, 3)):
            entries = chip_stats(par, t)
            for side in range(2):
                entries.append(tuple(st_r[u, side, 2 * i + row : 2 * i + row + 1, :] for row in range(2)))
            for row, value in enumerate(merge(entries)):
                ret_s[u, 2 * i + row : 2 * i + row + 1, :] = value
        for side in range(2):

            @pl.when(present[side])
            def _():
                remote(
                    ret_s.at[u], ret_r.at[u, 1 - side], side_s.at[side, 3], ret_rs.at[1 - side, u], peers[side]
                ).start()

    def factors(par, t, log_total, row_dot):
        for x in range(2):
            if (t, x) in ((0, 1), (5, 0)):
                continue
            j = 2 * t - x
            power = jnp.where(attended(t, x), mx[par, j, 0:1, :] - log_total, NEG)
            fr[j, 0:1, :] = jnp.exp2(power)
            fr[j, 1:2, :] = row_dot

    def second_pass(u, par, skip):
        h = lax.div(u, SPLIT)
        a = lax.rem(h, 2)

        def pair(j, carry):
            t, x = lax.div(j + 1, 2), lax.rem(j, 2)
            w = p[par, j] * fr[j, 0:1, :]
            low = w.astype(BF16)
            ds = (w * (gw[par, j] - fr[j, 1:2, :])).astype(BF16)
            acc[a, x, 1] += nn(low, qd[t, u, 1])
            acc[a, x, 0] += nn(ds, qd[t, u, 0])
            dqj[j - skip] = tn(ds, kv[h, x, 0])
            return carry

        return pair

    def start_unit(u, par):
        h = lax.div(u, SPLIT)

        @pl.when(lax.rem(u, SPLIT) == 0)
        def _():
            wait_bytes(kv.at[h, g], loc_s.at[1, h])
            wait_bytes(kv.at[h, 1 - g], kv_rs.at[h])

        @pl.when(u == 0)
        def _():
            wait_bytes(mk.at[3 - g], mk_rs.at[2])
            for side in range(2):

                @pl.when(present[side])
                def _():
                    for i, t in enumerate(theirs_t[side]):
                        wait_bytes(mk.at[t], mk_rs.at[3 * side + i])

        wait_bytes(qd.at[2 + g, u], loc_s.at[0, u])
        wait_bytes(qd.at[3 - g, u], qd_rs.at[2, u])
        pair = first_pass(u, par)
        lax.fori_loop(3, 7, pair, 0, unroll=True)
        wait_side(u, 0)
        lax.fori_loop(0, 3, pair, 0, unroll=True)
        send_stats(u, par, 0)
        wait_side(u, 1)
        lax.fori_loop(7, 10, pair, 0, unroll=True)
        send_stats(u, par, 1)

    def finish_local(u, par):
        h, half, rows = part(u)
        cols = head_cols(g, h)
        for i, t in enumerate((2, 3)):
            factors(par, t, ret_s[u, 2 * i : 2 * i + 1, :], ret_s[u, 2 * i + 1 : 2 * i + 2, :])
        lax.fori_loop(3, 7, second_pass(u, par, 3), 0, unroll=True)
        dq[rows, cols] = dqj[2 * g] + dqj[2 * g + 1]
        slot = lax.rem(u, DEPTH)

        @pl.when(u >= DEPTH)
        def _():
            wait_bytes(dqf.at[0], send_s.at[8 + slot])

        dqf[slot] = dqj[2 - 2 * g] + dqj[3 - 2 * g]
        remote(dqf.at[slot], dq.at[rows, cols], send_s.at[8 + slot], dq_rs.at[2, h], mate).start()

        @pl.when(half == SPLIT - 1)
        def _():
            a = lax.rem(h, 2)
            acc[a, :, 0] = acc[a, :, 0] * SCALE
            for i, out in enumerate((dk, dv)):
                out[:, cols] = acc[a, g, i]
                remote(
                    acc.at[a, 1 - g, i], out.at[:, cols], send_s.at[4 + 2 * a + i], out_rs.at[i], mate
                ).start()

    def open_head(u):
        h, half, _ = part(u)

        @pl.when(half == 0)
        def _():
            @pl.when(h >= 2)
            def _():
                for i in range(2):
                    wait_bytes(acc.at[0, 0, 0], send_s.at[4 + 2 * lax.rem(h, 2) + i])

            acc[lax.rem(h, 2)] = jnp.zeros((2, 2, BLK, HD), F32)

    def finish_remote(u, par):
        h, half, rows = part(u)
        cols = head_cols(g, h)
        slot = lax.rem(u, DEPTH)

        for side, first in enumerate((0, 7)):

            @pl.when(present[side])
            def _():
                wait_bytes(ret_r.at[u, side], ret_rs.at[side, u])

            for i, t in enumerate(theirs_t[side]):
                factors(par, t, ret_r[u, side, 2 * i : 2 * i + 1, :], ret_r[u, side, 2 * i + 1 : 2 * i + 2, :])
            lax.fori_loop(first, first + 3, second_pass(u, par, 4 * side), 0, unroll=True)
            @pl.when(jnp.logical_and(present[side], u >= DEPTH))
            def _():
                wait_bytes(dqb.at[0, 0], side_s.at[side, 4 + slot])

            if side == 0:
                dqb[slot, 0, 0] = dqj[0].astype(BF16)
                dqb[slot, 0, 1] = (dqj[1] + dqj[2]).astype(BF16)
            else:
                dqb[slot, 1, 0] = (dqj[3] + dqj[4]).astype(BF16)
                dqb[slot, 1, 1] = dqj[5].astype(BF16)

            @pl.when(present[side])
            def _():
                for core in range(2):
                    remote(
                        dqb.at[slot, side, core], dqr.at[1 - side, rows, cols], side_s.at[side, 4 + slot],
                        dq_rs.at[1 - side, h], chips[side][core],
                    ).start()

    def step(s, carry):
        @pl.when(s < U)
        def _():
            start_unit(s, lax.rem(s, DEPTH))

        @pl.when(s >= 2)
        def _():
            open_head(s - 2)

        @pl.when(s == U)
        def _():
            finish_local(s - 2, lax.rem(s - 2, DEPTH))

        @pl.when(jnp.logical_and(s >= 1, s < U + 1))
        def _():
            combine(s - 1, lax.rem(s - 1, DEPTH))

        @pl.when(s < U)
        def _():
            send_ahead(s, AHEAD)
            send_ahead(s, AHEAD + 1)

        @pl.when(s >= 2)
        def _():
            finish_remote(s - 2, lax.rem(s - 2, DEPTH))

        @pl.when(jnp.logical_and(s >= 2, s != U))
        def _():
            finish_local(s - 2, lax.rem(s - 2, DEPTH))

        return carry

    lax.fori_loop(0, U + 2, step, 0)

    theirs = pl.ds(pl.multiple_of((1 - g) * HG * HD, HD), HG * HD)
    for h in range(HG):
        for side in range(2):

            @pl.when(present[side])
            def _():
                wait_bytes(dqr.at[side, :, pl.ds(0, 2 * HD)], dq_rs.at[side, h])

        wait_bytes(dq.at[:, pl.ds(0, HD)], dq_rs.at[2, h])
        for core in range(2):
            cols = head_cols(core, h)

            def total(i, carry):
                rows = pl.ds(pl.multiple_of(i * 128, 128), 128)
                dq[rows, cols] = (
                    dq[rows, cols] + dqr[0, rows, cols].astype(F32) + dqr[1, rows, cols].astype(F32)
                ) * SCALE
                return carry

            lax.fori_loop(0, BLK // 128, total, 0, unroll=2)
    wait_bytes(qd.at[0], send_s.at[0])
    wait_bytes(kv.at[:, 0], send_s.at[1])
    wait_bytes(mk.at[0], send_s.at[2])
    for slot in range(DEPTH):
        wait_bytes(dqf.at[0], send_s.at[8 + slot])
    for i in range(4):
        wait_bytes(acc.at[0, 0, 0], send_s.at[4 + i])
    for side in range(2):

        @pl.when(present[side])
        def _():
            wait_bytes(qd.at[pl.ds(0, 2)], side_s.at[side, 0])
            wait_bytes(mk.at[pl.ds(0, 2)], side_s.at[side, 1])
            wait_bytes(st_s.at[:, 0], side_s.at[side, 2])
            wait_bytes(ret_s, side_s.at[side, 3])
            for slot in range(DEPTH):
                wait_bytes(dqb.at[0, 0], side_s.at[side, 4 + slot])

    wait_bytes(dk.at[:, theirs], out_rs.at[0])
    wait_bytes(dv.at[:, theirs], out_rs.at[1])


def write_out(dq, dk, dv, dq_out, dk_out, dv_out, sems):
    copies = [
        pltpu.make_async_copy(src, dst, sems.at[i])
        for i, (src, dst) in enumerate(((dq, dq_out), (dk, dk_out), (dv, dv_out)))
    ]
    for copy in copies:
        copy.start()
    for copy in copies:
        copy.wait()


def body(pb_size, kv_size, queries, keys, values, grad_out, offsets):
    rows, width = queries.shape
    any_space = pl.BlockSpec(memory_space=pl.ANY)
    vmem = pl.BlockSpec(memory_space=pltpu.VMEM)
    whole = jax.ShapeDtypeStruct((rows, width), F32)
    dma = pltpu.SemaphoreType.DMA
    in_hbm = [pltpu.with_memory_space_constraint(a, pltpu.HBM) for a in (queries, keys, values, grad_out, offsets)]
    grads = pl.pallas_call(
        functools.partial(kernel, pb_size, kv_size),
        out_shape=(whole,) * 3,
        in_specs=[any_space] * 5,
        out_specs=[vmem] * 3,
        scratch_shapes=[
            pltpu.VMEM((6, U, 2, R, HD), BF16),
            pltpu.VMEM((HG, 2, 2, BLK, HD), BF16),
            pltpu.VMEM((DEPTH, PAIRS, BLK, R), F32),
            pltpu.VMEM((DEPTH, PAIRS, BLK, R), F32),
            pltpu.VMEM((DEPTH, PAIRS, 8, R), F32),
            pltpu.VMEM((PAIRS, 8, R), F32),
            pltpu.VMEM((6, R, HD), F32),
            pltpu.VMEM((2, 2, 2, BLK, HD), F32),
            pltpu.VMEM((DEPTH, R, HD), F32),
            pltpu.VMEM((DEPTH, 2, 2, R, HD), BF16),
            pltpu.VMEM((2, BLK, 2 * HG * HD), BF16),
            pltpu.VMEM((U, 2, 4, R), F32),
            pltpu.VMEM((U, 2, 4, R), F32),
            pltpu.VMEM((U, 4, R), F32),
            pltpu.VMEM((U, 2, 4, R), F32),
            pltpu.VMEM((6, 8, R), F32),
            pltpu.SMEM((1, BAND), jnp.int32),
            dma((5, U)),
            dma((HG,)),
            dma((2, U)),
            dma((2, U)),
            dma((5,)),
            dma((2,)),
            dma((3, HG)),
            dma((8 + DEPTH,)),
            dma((2, 4 + DEPTH)),
            dma((2, U)),
            dma((1,)),
        ],
        compiler_params=pltpu.CompilerParams(
            collective_id=0, has_side_effects=True, vmem_limit_bytes=VMEM_LIMIT
        ),
        cost_estimate=pl.CostEstimate(flops=14 * 10**9, bytes_accessed=16 << 20, transcendentals=10 * 2**20),
        name="band_backward",
    )(*in_hbm)
    in_vmem = [pltpu.with_memory_space_constraint(a, pltpu.VMEM) for a in grads]
    return pl.pallas_call(
        write_out,
        out_shape=(whole,) * 3,
        in_specs=[any_space] * 3,
        out_specs=[any_space] * 3,
        scratch_shapes=[dma((3,))],
        compiler_params=pltpu.CompilerParams(vmem_limit_bytes=1 << 20),
        name="write_out",
    )(*in_vmem)


def solution(mesh):
    spec = P(("pb", "kv"), None)
    return jax.shard_map(
        functools.partial(body, mesh.shape["pb"], mesh.shape["kv"]),
        mesh=mesh,
        in_specs=(spec,) * 5,
        out_specs=(spec,) * 3,
        check_vma=False,
    )
```

```python
import functools
import math

import jax
import jax.numpy as jnp
from jax import lax
from jax.experimental import pallas as pl
from jax.experimental.pallas import tpu as pltpu
from jax.sharding import PartitionSpec as P

HEADS = 8
BAND = 5
HG = HEADS // 2
HD = 128
BLK = 512
R = 256
SPLIT = BLK // R
U = HG * SPLIT
PAIRS = 10
DEPTH = 3
NEG = -1e30
SCALE = HD**-0.5
C2 = SCALE * math.log2(math.e)
MESH = pl.DeviceIdType.MESH
F32, BF16 = jnp.float32, jnp.bfloat16
AHEAD = 4
VMEM_LIMIT = 47 << 20


def nt(a, b):
    return lax.dot_general(a, b, (((1,), (1,)), ((), ())), preferred_element_type=F32)


def nn(a, b):
    return lax.dot_general(a, b, (((1,), (0,)), ((), ())), preferred_element_type=F32)


def tn(a, b):
    return lax.dot_general(a, b, (((0,), (0,)), ((), ())), preferred_element_type=F32)


def kernel(
    pb_size, kv_size,
    q_ref, k_ref, v_ref, do_ref, off_ref,
    dq, dk, dv,
    qd, kv, p, gw, mx, fr, dqj, acc, dqf, dqb, dqr, st_s, st_r, ret_s, ret_r, mk, off,
    qd_rs, kv_rs, st_rs, ret_rs, mk_rs, out_rs, dq_rs, send_s, side_s, loc_s, off_s,
):
    n = pb_size * kv_size
    me = lax.axis_index("pb") * kv_size + lax.axis_index("kv")
    g = lax.rem(me, 2)
    base = me - g

    def dev(block):
        block = lax.rem(block + n, n)
        return (lax.div(block, kv_size), lax.rem(block, kv_size))

    present = (base > 0, base + 2 < n)
    mate = dev(base + 1 - g)
    chips = ([dev(base - 2), dev(base - 1)], [dev(base + 2), dev(base + 3)])
    peers = (dev(me - 2), dev(me + 2))
    slots = (4 + g, g)
    theirs_t = ((0, 1), (4, 5))

    def remote(src, dst, send, recv, to):
        return pltpu.make_async_remote_copy(
            src_ref=src, dst_ref=dst, send_sem=send, recv_sem=recv, device_id=to, device_id_type=MESH
        )

    def wait_bytes(ref, sem):
        pltpu.make_async_copy(ref, ref, sem).wait()

    def part(u):
        h, half = lax.div(u, SPLIT), lax.rem(u, SPLIT)
        return h, half, pl.ds(pl.multiple_of(half * R, R), R)

    def head_cols(core, h):
        return pl.ds(pl.multiple_of((core * HG + h) * HD, HD), HD)

    barrier = pltpu.get_barrier_semaphore()
    pl.semaphore_signal(barrier, inc=1, device_id=mate, device_id_type=MESH)
    for side in range(2):

        @pl.when(present[side])
        def _():
            for to in chips[side]:
                pl.semaphore_signal(barrier, inc=1, device_id=to, device_id_type=MESH)

    copy = pltpu.make_async_copy(off_ref, off, off_s.at[0])
    copy.start()
    copy.wait()
    for slot in range(8):
        if slot < BAND:
            flag = jnp.where(off[0, slot] != 3, 1.0, 0.0).astype(F32)
        else:
            flag = jnp.float32(0.0)
        mk[2 + g, slot : slot + 1, :] = jnp.full((1, R), flag, F32)

    def start_own(u, carry):
        h, _, rows = part(u)
        cols = head_cols(g, h)
        for i, ref in enumerate((q_ref, do_ref)):
            pltpu.make_async_copy(ref.at[rows, cols], qd.at[2 + g, u, i], loc_s.at[0, u]).start()
        return carry

    def start_own_kv(h, carry):
        cols = head_cols(g, h)
        for i, ref in enumerate((k_ref, v_ref)):
            pltpu.make_async_copy(ref.at[:, cols], kv.at[h, g, i], loc_s.at[1, h]).start()
        return carry

    def send_part(k):
        u, i = k
        h, _, rows = part(u)
        ref = (do_ref, q_ref)[i]
        cols = head_cols(1 - g, h)
        remote(ref.at[rows, cols], qd.at[2 + g, u, 1 - i], send_s.at[0], qd_rs.at[2, u], mate).start()
        for side in range(2):

            @pl.when(present[side])
            def _():
                for core in range(2):
                    remote(
                        ref.at[rows, head_cols(core, h)], qd.at[slots[side], u, 1 - i], side_s.at[side, 0],
                        qd_rs.at[(3 + g, g)[side], u], chips[side][core],
                    ).start()

    def send_ahead(s, k):
        u = s + k // 2

        @pl.when(u < U)
        def _():
            send_part((u, k % 2))

    def send_kv(h):
        cols = head_cols(1 - g, h)
        for i, ref in enumerate((k_ref, v_ref)):
            remote(ref.at[:, cols], kv.at[h, g, i], send_s.at[1], kv_rs.at[h], mate).start()

    lax.fori_loop(0, HG, start_own_kv, 0)
    lax.fori_loop(0, U, start_own, 0)

    for side in range(2):

        @pl.when(jnp.logical_not(present[side]))
        def _():
            def clear(u, carry):
                for t in theirs_t[side]:
                    qd[t, u] = jnp.zeros((2, R, HD), BF16)
                for row in range(4):
                    st_r[u, side, row : row + 1, :] = jnp.full((1, R), 0.0 if row % 2 else NEG, F32)
                ret_r[u, side] = jnp.zeros((4, R), F32)
                return carry

            lax.fori_loop(0, U, clear, 0)
            for t in theirs_t[side]:
                mk[t] = jnp.zeros((8, R), F32)
            dqr[side] = jnp.zeros((BLK, 2 * HG * HD), BF16)

    pl.semaphore_wait(barrier, 1 + 2 * sum(p_.astype(jnp.int32) for p_ in present))

    tile = mk.at[2 + g]
    remote(tile, tile, send_s.at[2], mk_rs.at[2], mate).start()
    for side in range(2):

        @pl.when(present[side])
        def _():
            for core in range(2):
                remote(
                    tile, mk.at[slots[side]], side_s.at[side, 1], mk_rs.at[(3 + g, g)[side]], chips[side][core]
                ).start()

    send_part((0, 0))
    send_part((0, 1))
    send_kv(0)
    for k in range(2, AHEAD):
        send_part((k // 2, k % 2))
    for h in range(1, HG):
        send_kv(h)

    def wait_side(u, side):
        @pl.when(present[side])
        def _():
            for i, t in enumerate(theirs_t[side]):
                wait_bytes(qd.at[t, u], qd_rs.at[3 * side + i, u])

    def first_pass(u, par):
        h = lax.div(u, SPLIT)

        def pair(j, carry):
            t, x = lax.div(j + 1, 2), lax.rem(j, 2)
            grads = nt(kv[h, x, 1], qd[t, u, 1])
            gw[par, j] = grads
            raw = nt(kv[h, x, 0], qd[t, u, 0])
            m = jnp.max(raw, axis=0, keepdims=True) * C2
            e = jnp.exp2(raw * C2 - m)
            p[par, j] = e
            mx[par, j, 0:1, :] = m
            mx[par, j, 1:2, :] = jnp.sum(e, axis=0, keepdims=True)
            mx[par, j, 2:3, :] = jnp.sum(e * grads, axis=0, keepdims=True)
            return carry

        return pair

    def attended(t, x):
        return mk[t, 4 - t + x : 5 - t + x, :] > 0.5

    def merge(entries):
        top = functools.reduce(jnp.maximum, [a for a, _ in entries])
        weights = [jnp.exp2(a - top) for a, _ in entries]
        total = sum(weights)
        return top + jnp.log2(total), sum(b * w for (_, b), w in zip(entries, weights)) / total

    def chip_stats(par, t):
        entries = []
        for x in range(2):
            if (t, x) in ((0, 1), (5, 0)):
                continue
            j = 2 * t - x
            on = attended(t, x)
            total = mx[par, j, 1:2, :]
            log_part = mx[par, j, 0:1, :] + jnp.log2(total)
            entries.append((jnp.where(on, log_part, NEG), jnp.where(on, mx[par, j, 2:3, :] / total, 0.0)))
        return entries

    def send_stats(u, par, side):
        for i, t in enumerate(theirs_t[side]):
            for row, value in enumerate(merge(chip_stats(par, t))):
                st_s[u, side, 2 * i + row : 2 * i + row + 1, :] = value

        @pl.when(present[side])
        def _():
            remote(
                st_s.at[u, side], st_r.at[u, 1 - side], side_s.at[side, 2], st_rs.at[1 - side, u], peers[side]
            ).start()

    def combine(u, par):
        for side in range(2):

            @pl.when(present[side])
            def _():
                wait_bytes(st_r.at[u, side], st_rs.at[side, u])

        for i, t in enumerate((2, 3)):
            entries = chip_stats(par, t)
            for side in range(2):
                entries.append(tuple(st_r[u, side, 2 * i + row : 2 * i + row + 1, :] for row in range(2)))
            for row, value in enumerate(merge(entries)):
                ret_s[u, 2 * i + row : 2 * i + row + 1, :] = value
        for side in range(2):

            @pl.when(present[side])
            def _():
                remote(
                    ret_s.at[u], ret_r.at[u, 1 - side], side_s.at[side, 3], ret_rs.at[1 - side, u], peers[side]
                ).start()

    def factors(par, t, log_total, row_dot):
        for x in range(2):
            if (t, x) in ((0, 1), (5, 0)):
                continue
            j = 2 * t - x
            power = jnp.where(attended(t, x), mx[par, j, 0:1, :] - log_total, NEG)
            fr[j, 0:1, :] = jnp.exp2(power)
            fr[j, 1:2, :] = row_dot

    def second_pass(u, par, skip):
        h = lax.div(u, SPLIT)
        a = lax.rem(h, 2)

        def pair(j, carry):
            t, x = lax.div(j + 1, 2), lax.rem(j, 2)
            w = p[par, j] * fr[j, 0:1, :]
            low = w.astype(BF16)
            ds = (w * (gw[par, j] - fr[j, 1:2, :])).astype(BF16)
            acc[a, x, 1] += nn(low, qd[t, u, 1])
            acc[a, x, 0] += nn(ds, qd[t, u, 0])
            dqj[j - skip] = tn(ds, kv[h, x, 0])
            return carry

        return pair

    def start_unit(u, par):
        h = lax.div(u, SPLIT)

        @pl.when(lax.rem(u, SPLIT) == 0)
        def _():
            wait_bytes(kv.at[h, g], loc_s.at[1, h])
            wait_bytes(kv.at[h, 1 - g], kv_rs.at[h])

        @pl.when(u == 0)
        def _():
            wait_bytes(mk.at[3 - g], mk_rs.at[2])
            for side in range(2):

                @pl.when(present[side])
                def _():
                    for i, t in enumerate(theirs_t[side]):
                        wait_bytes(mk.at[t], mk_rs.at[3 * side + i])

        wait_bytes(qd.at[2 + g, u], loc_s.at[0, u])
        wait_bytes(qd.at[3 - g, u], qd_rs.at[2, u])
        pair = first_pass(u, par)
        lax.fori_loop(3, 7, pair, 0, unroll=True)
        wait_side(u, 0)
        lax.fori_loop(0, 3, pair, 0, unroll=True)
        send_stats(u, par, 0)
        wait_side(u, 1)
        lax.fori_loop(7, 10, pair, 0, unroll=True)
        send_stats(u, par, 1)

    def finish_local(u, par):
        h, half, rows = part(u)
        cols = head_cols(g, h)
        for i, t in enumerate((2, 3)):
            factors(par, t, ret_s[u, 2 * i : 2 * i + 1, :], ret_s[u, 2 * i + 1 : 2 * i + 2, :])
        lax.fori_loop(3, 7, second_pass(u, par, 3), 0, unroll=True)
        dq[rows, cols] = dqj[2 * g] + dqj[2 * g + 1]
        slot = lax.rem(u, DEPTH)

        @pl.when(u >= DEPTH)
        def _():
            wait_bytes(dqf.at[0], send_s.at[8 + slot])

        dqf[slot] = dqj[2 - 2 * g] + dqj[3 - 2 * g]
        remote(dqf.at[slot], dq.at[rows, cols], send_s.at[8 + slot], dq_rs.at[2, h], mate).start()

        @pl.when(half == SPLIT - 1)
        def _():
            a = lax.rem(h, 2)
            acc[a, :, 0] = acc[a, :, 0] * SCALE
            for i, out in enumerate((dk, dv)):
                out[:, cols] = acc[a, g, i]
                remote(
                    acc.at[a, 1 - g, i], out.at[:, cols], send_s.at[4 + 2 * a + i], out_rs.at[i], mate
                ).start()

    def open_head(u):
        h, half, _ = part(u)

        @pl.when(half == 0)
        def _():
            @pl.when(h >= 2)
            def _():
                for i in range(2):
                    wait_bytes(acc.at[0, 0, 0], send_s.at[4 + 2 * lax.rem(h, 2) + i])

            acc[lax.rem(h, 2)] = jnp.zeros((2, 2, BLK, HD), F32)

    def finish_remote(u, par):
        h, half, rows = part(u)
        cols = head_cols(g, h)
        slot = lax.rem(u, DEPTH)

        for side, first in enumerate((0, 7)):

            @pl.when(present[side])
            def _():
                wait_bytes(ret_r.at[u, side], ret_rs.at[side, u])

            for i, t in enumerate(theirs_t[side]):
                factors(par, t, ret_r[u, side, 2 * i : 2 * i + 1, :], ret_r[u, side, 2 * i + 1 : 2 * i + 2, :])
            lax.fori_loop(first, first + 3, second_pass(u, par, 4 * side), 0, unroll=True)
            @pl.when(jnp.logical_and(present[side], u >= DEPTH))
            def _():
                wait_bytes(dqb.at[0, 0], side_s.at[side, 4 + slot])

            if side == 0:
                dqb[slot, 0, 0] = dqj[0].astype(BF16)
                dqb[slot, 0, 1] = (dqj[1] + dqj[2]).astype(BF16)
            else:
                dqb[slot, 1, 0] = (dqj[3] + dqj[4]).astype(BF16)
                dqb[slot, 1, 1] = dqj[5].astype(BF16)

            @pl.when(present[side])
            def _():
                for core in range(2):
                    remote(
                        dqb.at[slot, side, core], dqr.at[1 - side, rows, cols], side_s.at[side, 4 + slot],
                        dq_rs.at[1 - side, h], chips[side][core],
                    ).start()

    def step(s, carry):
        @pl.when(s < U)
        def _():
            start_unit(s, lax.rem(s, DEPTH))

        @pl.when(jnp.logical_and(s >= 1, s < U + 1))
        def _():
            combine(s - 1, lax.rem(s - 1, DEPTH))

        @pl.when(s < U)
        def _():
            send_ahead(s, AHEAD)
            send_ahead(s, AHEAD + 1)

        @pl.when(s >= 2)
        def _():
            open_head(s - 2)
            finish_remote(s - 2, lax.rem(s - 2, DEPTH))
            finish_local(s - 2, lax.rem(s - 2, DEPTH))

        return carry

    lax.fori_loop(0, U + 2, step, 0)

    theirs = pl.ds(pl.multiple_of((1 - g) * HG * HD, HD), HG * HD)
    for h in range(HG):
        for side in range(2):

            @pl.when(present[side])
            def _():
                wait_bytes(dqr.at[side, :, pl.ds(0, 2 * HD)], dq_rs.at[side, h])

        wait_bytes(dq.at[:, pl.ds(0, HD)], dq_rs.at[2, h])
        for core in range(2):
            cols = head_cols(core, h)

            def total(i, carry):
                rows = pl.ds(pl.multiple_of(i * 128, 128), 128)
                dq[rows, cols] = (
                    dq[rows, cols] + dqr[0, rows, cols].astype(F32) + dqr[1, rows, cols].astype(F32)
                ) * SCALE
                return carry

            lax.fori_loop(0, BLK // 128, total, 0, unroll=2)
    wait_bytes(qd.at[0], send_s.at[0])
    wait_bytes(kv.at[:, 0], send_s.at[1])
    wait_bytes(mk.at[0], send_s.at[2])
    for slot in range(DEPTH):
        wait_bytes(dqf.at[0], send_s.at[8 + slot])
    for i in range(4):
        wait_bytes(acc.at[0, 0, 0], send_s.at[4 + i])
    for side in range(2):

        @pl.when(present[side])
        def _():
            wait_bytes(qd.at[pl.ds(0, 2)], side_s.at[side, 0])
            wait_bytes(mk.at[pl.ds(0, 2)], side_s.at[side, 1])
            wait_bytes(st_s.at[:, 0], side_s.at[side, 2])
            wait_bytes(ret_s, side_s.at[side, 3])
            for slot in range(DEPTH):
                wait_bytes(dqb.at[0, 0], side_s.at[side, 4 + slot])

    wait_bytes(dk.at[:, theirs], out_rs.at[0])
    wait_bytes(dv.at[:, theirs], out_rs.at[1])


def write_out(dq, dk, dv, dq_out, dk_out, dv_out, sems):
    copies = [
        pltpu.make_async_copy(src, dst, sems.at[i])
        for i, (src, dst) in enumerate(((dq, dq_out), (dk, dk_out), (dv, dv_out)))
    ]
    for copy in copies:
        copy.start()
    for copy in copies:
        copy.wait()


def body(pb_size, kv_size, queries, keys, values, grad_out, offsets):
    rows, width = queries.shape
    any_space = pl.BlockSpec(memory_space=pl.ANY)
    vmem = pl.BlockSpec(memory_space=pltpu.VMEM)
    whole = jax.ShapeDtypeStruct((rows, width), F32)
    dma = pltpu.SemaphoreType.DMA
    in_hbm = [pltpu.with_memory_space_constraint(a, pltpu.HBM) for a in (queries, keys, values, grad_out, offsets)]
    grads = pl.pallas_call(
        functools.partial(kernel, pb_size, kv_size),
        out_shape=(whole,) * 3,
        in_specs=[any_space] * 5,
        out_specs=[vmem] * 3,
        scratch_shapes=[
            pltpu.VMEM((6, U, 2, R, HD), BF16),
            pltpu.VMEM((HG, 2, 2, BLK, HD), BF16),
            pltpu.VMEM((DEPTH, PAIRS, BLK, R), F32),
            pltpu.VMEM((DEPTH, PAIRS, BLK, R), F32),
            pltpu.VMEM((DEPTH, PAIRS, 8, R), F32),
            pltpu.VMEM((PAIRS, 8, R), F32),
            pltpu.VMEM((6, R, HD), F32),
            pltpu.VMEM((2, 2, 2, BLK, HD), F32),
            pltpu.VMEM((DEPTH, R, HD), F32),
            pltpu.VMEM((DEPTH, 2, 2, R, HD), BF16),
            pltpu.VMEM((2, BLK, 2 * HG * HD), BF16),
            pltpu.VMEM((U, 2, 4, R), F32),
            pltpu.VMEM((U, 2, 4, R), F32),
            pltpu.VMEM((U, 4, R), F32),
            pltpu.VMEM((U, 2, 4, R), F32),
            pltpu.VMEM((6, 8, R), F32),
            pltpu.SMEM((1, BAND), jnp.int32),
            dma((5, U)),
            dma((HG,)),
            dma((2, U)),
            dma((2, U)),
            dma((5,)),
            dma((2,)),
            dma((3, HG)),
            dma((8 + DEPTH,)),
            dma((2, 4 + DEPTH)),
            dma((2, U)),
            dma((1,)),
        ],
        compiler_params=pltpu.CompilerParams(
            collective_id=0, has_side_effects=True, vmem_limit_bytes=VMEM_LIMIT
        ),
        cost_estimate=pl.CostEstimate(flops=14 * 10**9, bytes_accessed=16 << 20, transcendentals=10 * 2**20),
        name="band_backward",
    )(*in_hbm)
    in_vmem = [pltpu.with_memory_space_constraint(a, pltpu.VMEM) for a in grads]
    return pl.pallas_call(
        write_out,
        out_shape=(whole,) * 3,
        in_specs=[any_space] * 3,
        out_specs=[any_space] * 3,
        scratch_shapes=[dma((3,))],
        compiler_params=pltpu.CompilerParams(vmem_limit_bytes=1 << 20),
        name="write_out",
    )(*in_vmem)


def solution(mesh):
    spec = P(("pb", "kv"), None)
    return jax.shard_map(
        functools.partial(body, mesh.shape["pb"], mesh.shape["kv"]),
        mesh=mesh,
        in_specs=(spec,) * 5,
        out_specs=(spec,) * 3,
        check_vma=False,
    )
```
